256 devices in a mesh: rows: 64 (over x, z, core), help: 4 (over y).
Axes of the slice: x: 4, y: 4, z: 8, core: 2. Of those that a mesh axis runs over, the one named last changes fastest.
Arguments:
- embeddings: bfloat16 [65536, 1024], P('rows'), may hold values from -192 to 192
- clusters: int32 [65536, 1], P('rows'), may hold values from 0 to 63; in each aligned block of 1024 rows (0 to 1023, 1024 to 2047, ...) at most 32 rows name the same one
Outputs:
- max_similarity: float32 [65536], P('rows')
The draws below stay inside these ranges and needn't reach their ends.
Inputs may be any that keep to these rules, and one draw needn't show every extreme that they name: `clusters`: among the 1024 rows of one index of rows no cluster appears more than 32 times, and some cluster appears exactly 32 times there; every cluster appears somewhere.
All inputs are finite; a program needn't handle non-finite values.
Results may differ from the reference program's by a relative error of at most 0.00048.
Values may be sent and summed in bfloat16 or wider, within the bound.
A program may use at most 64 MiB of HBM per device.

```python
import math
import jax
import jax.numpy as jnp
import numpy as np
from jax import lax

D = 1024
ROW_DEV = 1024
MOST = 32
CLUSTERS = 64
ROWS_ALL = 65536
N_ROWS = 64


def draw_embeddings(key, part):
    key = jax.random.fold_in(key, 7)
    pool_key, pick_key, noise_key, level_key, scale_key = jax.random.split(key, 5)
    pool_size = max(ROW_DEV // 4, 2)
    pool = jax.random.truncated_normal(pool_key, -4.0, 4.0, (pool_size, D), jnp.float32)
    picked = jax.random.randint(pick_key, (ROWS_ALL,), 0, pool_size)
    base_rows = pool[picked]
    noise_level = jnp.exp(jax.random.uniform(level_key, (ROWS_ALL, 1), jnp.float32, jnp.log(0.2), jnp.log(2.0)))
    noise = jax.random.truncated_normal(noise_key, -4.0, 4.0, (ROWS_ALL, D), jnp.float32)
    row_scale = jnp.exp(jax.random.uniform(scale_key, (ROWS_ALL, 1), jnp.float32, 0.0, jnp.log(10.0)))
    return (row_scale * (base_rows + noise_level * noise)).astype(jnp.bfloat16)


def routed_block(key, own, number, rows, number_of, top, bound, slope):
    order = jax.random.permutation(key, number_of)
    packed, ordinary = load_shares(number_of, rows * top, bound, slope, True), load_shares(number_of, rows * top, bound, slope, False)
    places = jnp.arange(number_of)

    def named(sizes, offset_by):
        used = int((sizes > 0).sum())
        fixed = max(1, used // 4)
        moved = fixed + (places - fixed + offset_by * (used - fixed)) % max(1, number_of - fixed)
        return jnp.zeros((number_of,), jnp.int32).at[order[jnp.where(places < fixed, places, moved)]].set(jnp.asarray(sizes, jnp.int32))

    sizes = jnp.where(number % 4 == 0, named(packed, number // 4), named(ordinary, number - number // 4 - 1))
    mixed = jax.random.permutation(jax.random.fold_in(own, 3), number_of)
    source_of, taker = mixed[0:number_of // 2 * 2:2], mixed[1:number_of // 2 * 2:2]
    slack = jnp.minimum(sizes[source_of] - 1, bound - sizes[taker]) // 2
    slack = jnp.where((source_of == order[0]) | (taker == order[0]) | (sizes[taker] == 0), 0, jnp.maximum(slack, 0))
    moved = jax.random.randint(jax.random.fold_in(own, 4), (number_of // 2,), 0, 1 << 20) % (slack + 1)
    sizes = sizes.at[source_of].add(-moved).at[taker].add(moved)
    labels = jnp.searchsorted(jnp.cumsum(sizes), jnp.arange(rows * top), side="right").astype(jnp.int32)
    listing = labels.reshape(top, rows).T
    listing = listing[jax.random.permutation(jax.random.fold_in(own, 1), rows)]
    offset_by = jax.random.randint(jax.random.fold_in(own, 2), (rows, 1), 0, top)
    return jnp.take_along_axis(listing, (jnp.arange(top)[None, :] + offset_by) % top, axis=1)


def load_shares(number_of, total, reach, slope, full):
    loads = [(1 << 20) // math.isqrt(rank ** slope) + 1 for rank in range(1, number_of + 1)]
    largest = reach if full else min(reach, max(-(-total // number_of), total * loads[0] // sum(loads)))
    least = 1 if total - largest >= number_of - 1 else 0
    given, spare = [largest] + [least] * (number_of - 1), total - largest - least * (number_of - 1)
    while spare > 0:
        candidates = [i for i in range(1, number_of) if given[i] < largest] or [i for i in range(1, number_of) if given[i] < reach]
        whole, remaining = sum([loads[i] for i in candidates]), spare
        for i in candidates:
            addition = min(reach - given[i], max(1, remaining * loads[i] // whole), spare)
            given[i] = given[i] + addition
            spare = spare - addition
    return np.array(given)


def setup_inputs(seed: int = 0) -> dict:
    arg_keys = jax.random.split(jax.random.key(seed), 3)
    embeddings = draw_embeddings(jax.random.fold_in(arg_keys[2], 71), 0)
    clusters_keys = jax.random.split(jax.random.fold_in(arg_keys[1], 1), ROWS_ALL // ROW_DEV)
    clusters_turns = jax.random.permutation(jax.random.fold_in(arg_keys[1], 3), ROWS_ALL // ROW_DEV)
    clusters = jax.vmap(lambda own, number: routed_block(jax.random.fold_in(arg_keys[1], 2), own, number, ROW_DEV, CLUSTERS, 1, MOST, 1))(clusters_keys, clusters_turns).reshape((ROWS_ALL, 1))
    return {"embeddings": embeddings, "clusters": clusters}


EPSILON = 1e-06

def unit_rows(embeddings):
    values = embeddings.astype(jnp.float32)
    scale_inv = lax.rsqrt(lax.optimization_barrier(jnp.sum(values * values, axis=1, keepdims=True)) + EPSILON)
    return (values * scale_inv).astype(jnp.bfloat16)

def reference(embeddings, clusters):
    normed = unit_rows(embeddings).astype(jnp.float32)
    cluster_ids = clusters[:, 0].astype(jnp.int32)
    total_rows = normed.shape[0]
    sort_order = jnp.argsort(cluster_ids, stable=True).astype(jnp.int32)
    sorted_rows = normed[sort_order]
    sorted_ids = cluster_ids[sort_order]
    back_window = N_ROWS * MOST
    padded_rows = jnp.concatenate([jnp.zeros((back_window, normed.shape[1]), normed.dtype), sorted_rows], axis=0)
    padded_ids = jnp.concatenate([jnp.full((back_window,), -1, jnp.int32), sorted_ids], axis=0)
    padded_order = jnp.concatenate([jnp.full((back_window,), -1, jnp.int32), sort_order], axis=0)

    def one_block(block_start):
        query_rows = lax.dynamic_slice_in_dim(sorted_rows, block_start, 512, 0)
        query_ids = lax.dynamic_slice_in_dim(sorted_ids, block_start, 512, 0)
        query_order = lax.dynamic_slice_in_dim(sort_order, block_start, 512, 0)
        key_rows = lax.dynamic_slice_in_dim(padded_rows, block_start, back_window + 512, 0)
        key_ids = lax.dynamic_slice_in_dim(padded_ids, block_start, back_window + 512, 0)
        key_order = lax.dynamic_slice_in_dim(padded_order, block_start, back_window + 512, 0)
        scores = jnp.dot(query_rows, key_rows.T, precision=lax.Precision.HIGHEST, preferred_element_type=jnp.float32)
        allowed = (key_ids[None, :] == query_ids[:, None]) & (key_order[None, :] < query_order[:, None])
        return lax.optimization_barrier(jnp.max(jnp.where(allowed, scores, -1.0), axis=1))
    starts = (jnp.arange(total_rows // 512) * 512).astype(jnp.int32)
    best_sorted = lax.map(one_block, starts).reshape(-1)
    return jnp.zeros((total_rows,), jnp.float32).at[sort_order].set(best_sorted)
```

```python
import jax
import jax.numpy as jnp
from jax import lax
from jax.experimental import pallas as pl
from jax.experimental.pallas import tpu as pltpu
from jax.sharding import PartitionSpec as P

EPSILON = 1e-06
MESH = pl.DeviceIdType.MESH
D = 1024
ROWS = 1024
MOST = 32
NX, NZ, NY, NK = 4, 8, 4, 2
GROUP = NX * NK
BLOCK = GROUP * MOST
ORDER = (0, 1, 7, 2, 6, 3, 5, 4)
OWNERS = (0, 5)
FLAG = 4.0
OFF = -16.0


def kernel(emb_hbm, ids_ref, out_ref, emb, send, stage, keys, acc, row_bias, best_lane, ranks,
           onehot, best, ret1, ret2, ret3,
           emb_sem, z_send, z_recv, x_send, x_recv, x_copy, r1_send, r1_recv, r2_send, r2_recv,
           r3_send, r3_recv):
    r = lax.axis_index("rows")
    y = lax.axis_index("help")
    x, z, core = r // 16, (r // 2) % 8, r % 2
    lane_group = x * 2 + core

    def z_peer(offset):
        return {"rows": (x * 8 + (z + offset) % 8) * 2 + core}

    def x_peer(group):
        return {"rows": ((group // 2) * 8 + z) * 2 + group % 2}

    load = pltpu.make_async_copy(emb_hbm, emb, emb_sem)
    load.start()

    barrier = pltpu.get_barrier_semaphore()
    for offset in range(1, NZ):
        pl.semaphore_signal(barrier, inc=1, device_id=z_peer(offset), device_id_type=MESH)
    for step in range(1, GROUP):
        pl.semaphore_signal(
            barrier, inc=1, device_id=x_peer((lane_group + step) % GROUP), device_id_type=MESH
        )
    for step in range(1, NY):
        pl.semaphore_signal(
            barrier, inc=1, device_id={"help": (y + step) % NY}, device_id_type=MESH
        )

    iota_c = lax.broadcasted_iota(jnp.int32, (64, 128), 0)
    for b in range(8):
        hot = jnp.where(iota_c == ids_ref[b:b + 1, :], 1.0, 0.0).astype(jnp.bfloat16)
        onehot[b * 64:(b + 1) * 64, :] = hot
    tri_row = lax.broadcasted_iota(jnp.int32, (128, 256), 0)
    tri_col = lax.broadcasted_iota(jnp.int32, (128, 256), 1)
    tri = jnp.where((tri_row < tri_col) | (tri_col >= 128), 1.0, 0.0).astype(jnp.bfloat16)
    before = jnp.dot(onehot[...], tri, preferred_element_type=jnp.float32)
    base = jnp.zeros((64, 128), jnp.float32)
    for b in range(8):
        hot = onehot[b * 64:(b + 1) * 64, :].astype(jnp.float32)
        seen = before[b * 64:(b + 1) * 64, :128] + base
        rank = jnp.sum(hot * seen, axis=0, keepdims=True)
        ranks[b:b + 1, :] = rank.astype(jnp.int32)
        base = base + before[b * 64:(b + 1) * 64, 128:]
    best_lane[0:64, :] = base
    local_id = ids_ref[...] - 16 * y
    slot = (((local_id // 2) - z + 8) % 8) * 64 + (local_id % 2) * 32 + ranks[...]
    slot = jnp.where((local_id >= 0) & (local_id < 16), slot, -1)

    load.wait()
    iota_slot = lax.broadcasted_iota(jnp.int32, (64, 128), 0)
    lane = lax.broadcasted_iota(jnp.int32, (32, 128), 1)
    sub = lax.broadcasted_iota(jnp.int32, (32, 128), 0)

    def z_copy(offset):
        return pltpu.make_async_remote_copy(
            send.at[offset], stage.at[(8 - offset) % 8], z_send.at[offset],
            z_recv.at[(8 - offset) % 8], device_id=z_peer(offset), device_id_type=MESH
        )

    for half in range(2):
        offsets = ORDER[4 * half:4 * half + 4]
        pick = jnp.concatenate(
            [
                jnp.concatenate(
                    [
                        jnp.where(iota_slot + o * 64 == slot[b:b + 1, :], 1.0, 0.0).astype(jnp.bfloat16)
                        for b in range(8)
                    ],
                    axis=1,
                )
                for o in offsets
            ],
            axis=0,
        )
        picked = jnp.dot(pick, emb[...], preferred_element_type=jnp.float32)
        scale = lax.rsqrt(jnp.sum(picked * picked, axis=1, keepdims=True) + EPSILON)
        normed = (picked * scale).astype(jnp.bfloat16)
        for n, o in enumerate(offsets):
            send[o] = normed[n * 64:(n + 1) * 64, :]
            for j in range(2):
                cluster = 16 * y + ((z + o) % 8) * 2 + j
                count = best_lane[pl.ds(cluster, 1), :]
                empty = sub.astype(jnp.float32) >= count
                head = normed[n * 64 + j * 32:n * 64 + (j + 1) * 32, :128].astype(jnp.float32)
                head = jnp.where(empty & (lane == 0), FLAG, head)
                send[o, j * 32:(j + 1) * 32, 0:128] = head.astype(jnp.bfloat16)
        if half == 0:
            pl.semaphore_wait(barrier, NZ - 1 + GROUP - 1 + NY - 1)
        for o in offsets:
            if o:
                z_copy(o).start()

    def x_source(t, j):
        ref = send.at[0] if t == 0 else stage.at[ORDER[t]]
        return ref.at[pl.ds(j * 32, 32)]

    def x_target(t):
        return keys.at[t, pl.ds(pl.multiple_of(lane_group * 32, 32), 32)]

    def x_remote(t, j):
        return pltpu.make_async_remote_copy(
            x_source(t, j), x_target(t), x_send.at[t, j], x_recv.at[t],
            device_id=x_peer(OWNERS[j]), device_id_type=MESH
        )

    def x_local(t, j):
        return pltpu.make_async_copy(x_source(t, j), x_target(t), x_copy.at[t])

    def forward(t):
        if t:
            z_copy((8 - ORDER[t]) % 8).wait_recv()
        for j in range(2):
            @pl.when(lane_group == OWNERS[j])
            def _():
                x_local(t, j).start()

            @pl.when(lane_group != OWNERS[j])
            def _():
                x_remote(t, j).start()

    is_owner = (lane_group == OWNERS[0]) | (lane_group == OWNERS[1])
    lanes256 = lax.broadcasted_iota(jnp.int32, (1, 256), 1)
    dims = (((1,), (1,)), ((), ()))

    def compute(t):
        x_local(t, 0).wait()
        pltpu.make_async_remote_copy(
            keys.at[t, pl.ds(0, 224)], keys.at[t, pl.ds(0, 224)], x_send.at[0, 0], x_recv.at[t],
            device_id=x_peer(0), device_id_type=MESH
        ).wait_recv()
        new = keys[t]
        z_new = (z + ORDER[t]) % 8
        flags = keys[t, :, 0:128].astype(jnp.float32)
        bias = jnp.where(flags[:, 0:1] > 2.0, OFF, 0.0)
        row_bias[t] = jnp.broadcast_to(bias, (256, 128))
        first = jnp.where(lax.broadcasted_iota(jnp.int32, (16, 128), 1) == 0, 1.0, 0.0)
        lane_flag = lax.dot_general(
            first.astype(jnp.bfloat16), keys[t, :, 0:128], dims, preferred_element_type=jnp.float32
        )[0:1, :]
        lane_bias = jnp.where(lane_flag > 2.0, OFF, 0.0)
        scores = lax.dot_general(new, new, dims, preferred_element_type=jnp.float32)
        key_i = lax.broadcasted_iota(jnp.int32, (256, 256), 0)
        query_i = lax.broadcasted_iota(jnp.int32, (256, 256), 1)
        bias2 = jnp.concatenate([row_bias[t], row_bias[t]], axis=1)
        scores = jnp.where(key_i < query_i, scores + bias2, OFF)
        top = jnp.max(scores.reshape(32, 8, 256), axis=0)
        for u in range(t):
            z_old = (z + ORDER[u]) % 8
            shift = jnp.where(z_old < z_new, 0, 64)
            scores = lax.dot_general(keys[u], new, dims, preferred_element_type=jnp.float32)
            bias2 = jnp.concatenate([row_bias[u], row_bias[u]], axis=1)
            for g in range(4):
                new_later = lanes256 >= 64 * g + shift
                part = scores[64 * g:64 * (g + 1), :]
                down = part + bias2[64 * g:64 * (g + 1), :] + jnp.where(new_later, 0.0, OFF)
                top = jnp.maximum(top, jnp.max(down.reshape(8, 8, 256), axis=0))
                across = part + (lane_bias + jnp.where(new_later, OFF, 0.0))
                across = jnp.maximum(across[:, :128], across[:, 128:])
                rows = pl.ds(64 * g, 64)
                if u == t - 1:
                    acc[u, rows, :] = across
                else:
                    acc[u, rows, :] = jnp.maximum(acc[u, rows, :], across)
        best_lane[64 + t:65 + t, :] = jnp.max(top[:, :128], axis=0, keepdims=True)
        best_lane[72 + t:73 + t, :] = jnp.max(top[:, 128:], axis=0, keepdims=True)

    @pl.when(is_owner)
    def _():
        forward(0)
        for t in range(NZ):
            if t + 1 < NZ:
                forward(t + 1)
            compute(t)
        for h in range(2):
            for t in range(NZ):
                row = jnp.maximum(best_lane[64 + 8 * h + t:65 + 8 * h + t, :], -1.0)
                if t < NZ - 1:
                    turned = acc[t, h * 128:(h + 1) * 128, :].T
                    row = jnp.maximum(row, jnp.max(turned, axis=0, keepdims=True))
                best[h, t] = row

    @pl.when(jnp.logical_not(is_owner))
    def _():
        for t in range(NZ):
            forward(t)

    def back1(j, group):
        return pltpu.make_async_remote_copy(
            best.at[group // 4], ret1.at[j], r1_send.at[group], r1_recv.at[j],
            device_id=x_peer(group), device_id_type=MESH
        )

    for j in range(2):
        @pl.when(lane_group == OWNERS[j])
        def _():
            for group in range(GROUP):
                if group != OWNERS[j]:
                    back1(j, group).start()
            ret1[j] = best[OWNERS[j] // 4]

    for j in range(2):
        @pl.when(lane_group != OWNERS[j])
        def _():
            back1(j, 0).wait_recv()

    def back2(t):
        return pltpu.make_async_remote_copy(
            ret1.at[:, t], ret2.at[z], r2_send.at[t], r2_recv.at[(8 - ORDER[t]) % 8],
            device_id=z_peer(ORDER[t]), device_id_type=MESH
        )

    for t in range(1, NZ):
        back2(t).start()
    ret2[z] = ret1[:, 0]
    for t in range(1, NZ):
        pltpu.make_async_remote_copy(
            ret1.at[:, t], ret2.at[(z + ORDER[t]) % 8], r2_send.at[t], r2_recv.at[ORDER[t]],
            device_id=z_peer(ORDER[t]), device_id_type=MESH
        ).wait_recv()

    def back3(step):
        return pltpu.make_async_remote_copy(
            ret2, ret3.at[y], r3_send.at[step], r3_recv.at[(4 - step) % 4],
            device_id={"help": (y + step) % NY}, device_id_type=MESH
        )

    for step in range(1, NY):
        back3(step).start()
    ret3[y] = ret2[...]
    for step in range(1, NY):
        pltpu.make_async_remote_copy(
            ret2, ret3.at[(y + step) % NY], r3_send.at[step], r3_recv.at[step],
            device_id={"help": (y + step) % NY}, device_id_type=MESH
        ).wait_recv()

    values = ret3[...].reshape(64, 128)
    high = values.astype(jnp.bfloat16)
    rest = values - high.astype(jnp.float32)
    mid = rest.astype(jnp.bfloat16)
    low = (rest - mid.astype(jnp.float32)).astype(jnp.bfloat16)
    parts = jnp.concatenate([high, mid, low], axis=0)
    iota_lane = lax.broadcasted_iota(jnp.int32, (128, 128), 0)
    for b in range(8):
        hot = onehot[b * 64:(b + 1) * 64, :]
        hot3 = jnp.concatenate([hot, hot, hot], axis=0)
        table = lax.dot_general(
            parts, hot3, (((0,), (0,)), ((), ())), preferred_element_type=jnp.float32
        )
        want = ranks[b:b + 1, :] + (lane_group % 4) * 32
        out_ref[b:b + 1, :] = jnp.sum(jnp.where(iota_lane == want, table, 0.0), axis=0, keepdims=True)

    for offset in range(1, NZ):
        z_copy(offset).wait_send()
    for t in range(NZ):
        for j in range(2):
            @pl.when(lane_group != OWNERS[j])
            def _():
                x_remote(t, j).wait_send()
    for j in range(2):
        @pl.when(lane_group == OWNERS[j])
        def _():
            for group in range(GROUP):
                if group != OWNERS[j]:
                    back1(j, group).wait_send()
    for t in range(1, NZ):
        back2(t).wait_send()
    for step in range(1, NY):
        back3(step).wait_send()


def local(embeddings, clusters):
    dma = pltpu.SemaphoreType.DMA
    vmem = pltpu.VMEM
    out = pl.pallas_call(
        kernel,
        out_shape=jax.ShapeDtypeStruct((8, 128), jnp.float32),
        in_specs=[
            pl.BlockSpec(memory_space=pltpu.HBM),
            pl.BlockSpec(memory_space=pltpu.VMEM),
        ],
        out_specs=pl.BlockSpec(memory_space=pltpu.VMEM),
        scratch_shapes=[
            vmem((ROWS, D), jnp.bfloat16),
            vmem((NZ, 64, D), jnp.bfloat16),
            vmem((NZ, 64, D), jnp.bfloat16),
            vmem((NZ, BLOCK, D), jnp.bfloat16),
            vmem((NZ, BLOCK, 128), jnp.float32),
            vmem((NZ, BLOCK, 128), jnp.float32),
            vmem((80, 128), jnp.float32),
            vmem((8, 128), jnp.int32),
            vmem((512, 128), jnp.bfloat16),
            vmem((2, NZ, 1, 128), jnp.float32),
            vmem((2, NZ, 1, 128), jnp.float32),
            vmem((NZ, 2, 1, 128), jnp.float32),
            vmem((NY, NZ, 2, 1, 128), jnp.float32),
            dma,
            dma((NZ,)),
            dma((NZ,)),
            dma((NZ, 2)),
            dma((NZ,)),
            dma((NZ,)),
            dma((GROUP,)),
            dma((2,)),
            dma((NZ,)),
            dma((NZ,)),
            dma((NY,)),
            dma((NY,)),
        ],
        compiler_params=pltpu.CompilerParams(
            collective_id=0, has_side_effects=True, vmem_limit_bytes=48 << 20
        ),
    )(embeddings, clusters.reshape(8, 128))
    return out.reshape(ROWS)


def solution(mesh):
    placed = (P("rows", None), P("rows", None))
    return jax.shard_map(local, mesh=mesh, in_specs=placed, out_specs=P("rows"), check_vma=False)
```

```python
import jax
import jax.numpy as jnp
from jax import lax
from jax.experimental import pallas as pl
from jax.experimental.pallas import tpu as pltpu
from jax.sharding import PartitionSpec as P

EPSILON = 1e-06
MESH = pl.DeviceIdType.MESH
D = 1024
ROWS = 1024
MOST = 32
NX, NZ, NY, NK = 4, 8, 4, 2
GROUP = NX * NK
BLOCK = GROUP * MOST
ORDER = (0, 1, 7, 2, 6, 3, 5, 4)
OWNERS = (0, 5)
FLAG = 4.0
OFF = -16.0


def kernel(emb_hbm, ids_ref, out_ref, emb, send, stage, keys, acc, row_bias, best_lane, ranks,
           onehot, best, table,
           emb_sem, z_send, z_recv, x_send, x_recv, x_copy, back_send, back_recv):
    r = lax.axis_index("rows")
    y = lax.axis_index("help")
    x, z, core = r // 16, (r // 2) % 8, r % 2
    lane_group = x * 2 + core

    def z_peer(offset):
        return {"rows": (x * 8 + (z + offset) % 8) * 2 + core}

    def x_peer(group):
        return {"rows": ((group // 2) * 8 + z) * 2 + group % 2}

    load = pltpu.make_async_copy(emb_hbm, emb, emb_sem)
    load.start()

    barrier = pltpu.get_barrier_semaphore()
    for offset in range(1, NZ):
        pl.semaphore_signal(barrier, inc=1, device_id=z_peer(offset), device_id_type=MESH)
    for step in range(1, GROUP):
        pl.semaphore_signal(
            barrier, inc=1, device_id=x_peer((lane_group + step) % GROUP), device_id_type=MESH
        )
    for step in range(1, NY):
        pl.semaphore_signal(
            barrier, inc=1, device_id={"help": (y + step) % NY}, device_id_type=MESH
        )

    iota_c = lax.broadcasted_iota(jnp.int32, (64, 128), 0)
    for b in range(8):
        hot = jnp.where(iota_c == ids_ref[b:b + 1, :], 1.0, 0.0).astype(jnp.bfloat16)
        onehot[b * 64:(b + 1) * 64, :] = hot
    tri_row = lax.broadcasted_iota(jnp.int32, (128, 256), 0)
    tri_col = lax.broadcasted_iota(jnp.int32, (128, 256), 1)
    tri = jnp.where((tri_row < tri_col) | (tri_col >= 128), 1.0, 0.0).astype(jnp.bfloat16)
    before = jnp.dot(onehot[...], tri, preferred_element_type=jnp.float32)
    base = jnp.zeros((64, 128), jnp.float32)
    for b in range(8):
        hot = onehot[b * 64:(b + 1) * 64, :].astype(jnp.float32)
        seen = before[b * 64:(b + 1) * 64, :128] + base
        rank = jnp.sum(hot * seen, axis=0, keepdims=True)
        ranks[b:b + 1, :] = rank.astype(jnp.int32)
        base = base + before[b * 64:(b + 1) * 64, 128:]
    best_lane[0:64, :] = base
    local_id = ids_ref[...] - 16 * y
    slot = (((local_id // 2) - z + 8) % 8) * 64 + (local_id % 2) * 32 + ranks[...]
    slot = jnp.where((local_id >= 0) & (local_id < 16), slot, -1)

    load.wait()
    iota_slot = lax.broadcasted_iota(jnp.int32, (64, 128), 0)
    lane = lax.broadcasted_iota(jnp.int32, (32, 128), 1)
    sub = lax.broadcasted_iota(jnp.int32, (32, 128), 0)

    def z_copy(offset):
        return pltpu.make_async_remote_copy(
            send.at[offset], stage.at[(8 - offset) % 8], z_send.at[offset],
            z_recv.at[(8 - offset) % 8], device_id=z_peer(offset), device_id_type=MESH
        )

    for half in range(2):
        offsets = ORDER[4 * half:4 * half + 4]
        pick = jnp.concatenate(
            [
                jnp.concatenate(
                    [
                        jnp.where(iota_slot + o * 64 == slot[b:b + 1, :], 1.0, 0.0).astype(jnp.bfloat16)
                        for b in range(8)
                    ],
                    axis=1,
                )
                for o in offsets
            ],
            axis=0,
        )
        picked = jnp.dot(pick, emb[...], preferred_element_type=jnp.float32)
        scale = lax.rsqrt(jnp.sum(picked * picked, axis=1, keepdims=True) + EPSILON)
        normed = (picked * scale).astype(jnp.bfloat16)
        for n, o in enumerate(offsets):
            send[o] = normed[n * 64:(n + 1) * 64, :]
            for j in range(2):
                cluster = 16 * y + ((z + o) % 8) * 2 + j
                count = best_lane[pl.ds(cluster, 1), :]
                empty = sub.astype(jnp.float32) >= count
                head = normed[n * 64 + j * 32:n * 64 + (j + 1) * 32, :128].astype(jnp.float32)
                head = jnp.where(empty & (lane == 0), FLAG, head)
                send[o, j * 32:(j + 1) * 32, 0:128] = head.astype(jnp.bfloat16)
        if half == 0:
            pl.semaphore_wait(barrier, NZ - 1 + GROUP - 1 + NY - 1)
        for o in offsets:
            if o:
                z_copy(o).start()

    def x_source(t, j):
        ref = send.at[0] if t == 0 else stage.at[ORDER[t]]
        return ref.at[pl.ds(j * 32, 32)]

    def x_target(t):
        return keys.at[t, pl.ds(pl.multiple_of(lane_group * 32, 32), 32)]

    def x_remote(t, j):
        return pltpu.make_async_remote_copy(
            x_source(t, j), x_target(t), x_send.at[t, j], x_recv.at[t],
            device_id=x_peer(OWNERS[j]), device_id_type=MESH
        )

    def x_local(t, j):
        return pltpu.make_async_copy(x_source(t, j), x_target(t), x_copy.at[t])

    def forward(t):
        if t:
            z_copy((8 - ORDER[t]) % 8).wait_recv()
        for j in range(2):
            @pl.when(lane_group == OWNERS[j])
            def _():
                x_local(t, j).start()

            @pl.when(lane_group != OWNERS[j])
            def _():
                x_remote(t, j).start()

    is_owner = (lane_group == OWNERS[0]) | (lane_group == OWNERS[1])
    lanes256 = lax.broadcasted_iota(jnp.int32, (1, 256), 1)
    dims = (((1,), (1,)), ((), ()))

    def compute(t):
        x_local(t, 0).wait()
        pltpu.make_async_remote_copy(
            keys.at[t, pl.ds(0, 224)], keys.at[t, pl.ds(0, 224)], x_send.at[0, 0], x_recv.at[t],
            device_id=x_peer(0), device_id_type=MESH
        ).wait_recv()
        new = keys[t]
        z_new = (z + ORDER[t]) % 8
        flags = keys[t, :, 0:128].astype(jnp.float32)
        bias = jnp.where(flags[:, 0:1] > 2.0, OFF, 0.0)
        row_bias[t] = jnp.broadcast_to(bias, (256, 128))
        first = jnp.where(lax.broadcasted_iota(jnp.int32, (16, 128), 1) == 0, 1.0, 0.0)
        lane_flag = lax.dot_general(
            first.astype(jnp.bfloat16), keys[t, :, 0:128], dims, preferred_element_type=jnp.float32
        )[0:1, :]
        lane_bias = jnp.where(lane_flag > 2.0, OFF, 0.0)
        scores = lax.dot_general(new, new, dims, preferred_element_type=jnp.float32)
        key_i = lax.broadcasted_iota(jnp.int32, (256, 256), 0)
        query_i = lax.broadcasted_iota(jnp.int32, (256, 256), 1)
        bias2 = jnp.concatenate([row_bias[t], row_bias[t]], axis=1)
        scores = jnp.where(key_i < query_i, scores + bias2, OFF)
        top = jnp.max(scores.reshape(32, 8, 256), axis=0)
        for u in range(t):
            z_old = (z + ORDER[u]) % 8
            shift = jnp.where(z_old < z_new, 0, 64)
            scores = lax.dot_general(keys[u], new, dims, preferred_element_type=jnp.float32)
            bias2 = jnp.concatenate([row_bias[u], row_bias[u]], axis=1)
            for g in range(4):
                new_later = lanes256 >= 64 * g + shift
                part = scores[64 * g:64 * (g + 1), :]
                down = part + bias2[64 * g:64 * (g + 1), :] + jnp.where(new_later, 0.0, OFF)
                top = jnp.maximum(top, jnp.max(down.reshape(8, 8, 256), axis=0))
                across = part + (lane_bias + jnp.where(new_later, OFF, 0.0))
                across = jnp.maximum(across[:, :128], across[:, 128:])
                rows = pl.ds(64 * g, 64)
                if u == t - 1:
                    acc[u, rows, :] = across
                else:
                    acc[u, rows, :] = jnp.maximum(acc[u, rows, :], across)
        best_lane[64 + t:65 + t, :] = jnp.max(top[:, :128], axis=0, keepdims=True)
        best_lane[72 + t:73 + t, :] = jnp.max(top[:, 128:], axis=0, keepdims=True)

    @pl.when(is_owner)
    def _():
        forward(0)
        for t in range(NZ):
            if t + 1 < NZ:
                forward(t + 1)
            compute(t)
        for h in range(2):
            for t in range(NZ):
                row = jnp.maximum(best_lane[64 + 8 * h + t:65 + 8 * h + t, :], -1.0)
                if t < NZ - 1:
                    turned = acc[t, h * 128:(h + 1) * 128, :].T
                    row = jnp.maximum(row, jnp.max(turned, axis=0, keepdims=True))
                best[h, ORDER[t]] = row

    @pl.when(jnp.logical_not(is_owner))
    def _():
        for t in range(NZ):
            forward(t)

    def back(cluster, offset, step):
        group = (lane_group + step) % GROUP
        return pltpu.make_async_remote_copy(
            best.at[group // 4, offset], table.at[cluster], back_send, back_recv,
            device_id={
                "rows": ((group // 2) * 8 + (z + offset) % 8) * 2 + group % 2,
                "help": (y + 2 - step // GROUP + NY) % NY,
            },
            device_id_type=MESH,
        )

    for j in range(2):
        @pl.when(lane_group == OWNERS[j])
        def _():
            cluster = 16 * y + 2 * z + j
            for offset in (4, 3, 5, 2, 6, 1, 7, 0):
                for step in range(32):
                    if step != 16 or offset != 0:
                        back(cluster, offset, step).start()
            table[cluster] = best[OWNERS[j] // 4, 0]
            pltpu.make_async_remote_copy(
                table.at[pl.ds(0, 63)], table.at[pl.ds(0, 63)], back_send, back_recv,
                device_id=x_peer(0), device_id_type=MESH
            ).wait_recv()

    @pl.when(jnp.logical_not(is_owner))
    def _():
        pltpu.make_async_remote_copy(
            table.at[pl.ds(0, 64)], table.at[pl.ds(0, 64)], back_send, back_recv,
            device_id=x_peer(0), device_id_type=MESH
        ).wait_recv()

    values = table[0:64].reshape(64, 128)
    high = values.astype(jnp.bfloat16)
    rest = values - high.astype(jnp.float32)
    mid = rest.astype(jnp.bfloat16)
    low = (rest - mid.astype(jnp.float32)).astype(jnp.bfloat16)
    parts = jnp.concatenate([high, mid, low], axis=0)
    iota_lane = lax.broadcasted_iota(jnp.int32, (128, 128), 0)
    for b in range(8):
        hot = onehot[b * 64:(b + 1) * 64, :]
        hot3 = jnp.concatenate([hot, hot, hot], axis=0)
        looked = lax.dot_general(
            parts, hot3, (((0,), (0,)), ((), ())), preferred_element_type=jnp.float32
        )
        want = ranks[b:b + 1, :] + (lane_group % 4) * 32
        out_ref[b:b + 1, :] = jnp.sum(jnp.where(iota_lane == want, looked, 0.0), axis=0, keepdims=True)

    for offset in range(1, NZ):
        z_copy(offset).wait_send()
    for t in range(NZ):
        for j in range(2):
            @pl.when(lane_group != OWNERS[j])
            def _():
                x_remote(t, j).wait_send()
    @pl.when(is_owner)
    def _():
        pltpu.make_async_remote_copy(
            table.at[pl.ds(0, 255)], table.at[pl.ds(0, 255)], back_send, back_recv,
            device_id=x_peer(0), device_id_type=MESH
        ).wait_send()


def local(embeddings, clusters):
    dma = pltpu.SemaphoreType.DMA
    vmem = pltpu.VMEM
    out = pl.pallas_call(
        kernel,
        out_shape=jax.ShapeDtypeStruct((8, 128), jnp.float32),
        in_specs=[
            pl.BlockSpec(memory_space=pltpu.HBM),
            pl.BlockSpec(memory_space=pltpu.VMEM),
        ],
        out_specs=pl.BlockSpec(memory_space=pltpu.VMEM),
        scratch_shapes=[
            vmem((ROWS, D), jnp.bfloat16),
            vmem((NZ, 64, D), jnp.bfloat16),
            vmem((NZ, 64, D), jnp.bfloat16),
            vmem((NZ, BLOCK, D), jnp.bfloat16),
            vmem((NZ, BLOCK, 128), jnp.float32),
            vmem((NZ, BLOCK, 128), jnp.float32),
            vmem((80, 128), jnp.float32),
            vmem((8, 128), jnp.int32),
            vmem((512, 128), jnp.bfloat16),
            vmem((2, NZ, 1, 128), jnp.float32),
            vmem((256, 1, 128), jnp.float32),
            dma,
            dma((NZ,)),
            dma((NZ,)),
            dma((NZ, 2)),
            dma((NZ,)),
            dma((NZ,)),
            dma,
            dma,
        ],
        compiler_params=pltpu.CompilerParams(
            collective_id=0, has_side_effects=True, vmem_limit_bytes=60 << 20
        ),
    )(embeddings, clusters.reshape(8, 128))
    return out.reshape(ROWS)


def solution(mesh):
    placed = (P("rows", None), P("rows", None))
    return jax.shard_map(local, mesh=mesh, in_specs=placed, out_specs=P("rows"), check_vma=False)
```

```python
import jax
import jax.numpy as jnp
from jax import lax
from jax.experimental import pallas as pl
from jax.experimental.pallas import tpu as pltpu
from jax.sharding import PartitionSpec as P

EPSILON = 1e-06
MESH = pl.DeviceIdType.MESH
D = 1024
ROWS = 1024
MOST = 32
NX, NZ, NY, NK = 4, 8, 4, 2
GROUP = NX * NK
BLOCK = GROUP * MOST
ORDER = (0, 1, 7, 2, 6, 3, 5, 4)
FLAG = 4.0
OFF = -16.0


def kernel(emb_hbm, ids_ref, out_ref, emb, send, keys, acc, row_bias, best_lane, ranks,
           onehot, best, table,
           emb_sem, out_sem, in_sem, own_sem, back_send, back_recv):
    r = lax.axis_index("rows")
    y = lax.axis_index("help")
    x, z, core = r // 16, (r // 2) % 8, r % 2
    lane_group = x * 2 + core

    side = (y + 3 - 2 * core) % NY

    def owner_core(x_owner):
        return x_owner // 2

    is_owner = ((x + y + z) % 2 == 0) & (core == owner_core(x))

    def device(x_to, z_to, core_to, y_to):
        return {"rows": (x_to * 8 + z_to) * 2 + core_to, "help": y_to}

    load = pltpu.make_async_copy(emb_hbm, emb, emb_sem)
    load.start()

    barrier = pltpu.get_barrier_semaphore()
    @pl.when(is_owner)
    def _():
        for offset in (4, 3, 5, 2, 6, 1, 7, 0):
            z_to = (z + offset) % 8
            for step in range(NX):
                x_to = (x + 2 + step) % NX
                for core_to in range(NK):
                    @pl.when((offset != 0) | (step != 2) | (core_to != core))
                    def _():
                        pl.semaphore_signal(
                            barrier, inc=1, device_id=device(x_to, z_to, core_to, y),
                            device_id_type=MESH
                        )

                    pl.semaphore_signal(
                        barrier, inc=1,
                        device_id=device(x_to, z_to, core_to, (y + 1 + 2 * core_to) % NY),
                        device_id_type=MESH
                    )

    for step in range(1, NY):
        pl.semaphore_signal(
            barrier, inc=1, device_id={"help": (y + step) % NY}, device_id_type=MESH
        )

    iota_c = lax.broadcasted_iota(jnp.int32, (64, 128), 0)
    for b in range(8):
        hot = jnp.where(iota_c == ids_ref[b:b + 1, :], 1.0, 0.0).astype(jnp.bfloat16)
        onehot[b * 64:(b + 1) * 64, :] = hot
    tri_row = lax.broadcasted_iota(jnp.int32, (128, 256), 0)
    tri_col = lax.broadcasted_iota(jnp.int32, (128, 256), 1)
    tri = jnp.where((tri_row < tri_col) | (tri_col >= 128), 1.0, 0.0).astype(jnp.bfloat16)
    before = jnp.dot(onehot[...], tri, preferred_element_type=jnp.float32)
    base = jnp.zeros((64, 128), jnp.float32)
    for b in range(8):
        hot = onehot[b * 64:(b + 1) * 64, :].astype(jnp.float32)
        seen = before[b * 64:(b + 1) * 64, :128] + base
        rank = jnp.sum(hot * seen, axis=0, keepdims=True)
        ranks[b:b + 1, :] = rank.astype(jnp.int32)
        base = base + before[b * 64:(b + 1) * 64, 128:]
    best_lane[0:64, :] = base
    ids = ids_ref[...]
    plane, z_to, x_to = ids // 16, (ids // 2) % 8, (ids % 2) * 2 + (ids // 2 + ids // 16) % 2
    low = ranks[...] < 16
    slot = ((z_to - z + 8) % 8) * 64 + ((x_to - x + 4) % 4) * 16 + ranks[...] % 16
    slot = jnp.where(plane == jnp.where(low, y, side), slot, -1)

    load.wait()
    iota_slot = lax.broadcasted_iota(jnp.int32, (64, 128), 0)
    lane = lax.broadcasted_iota(jnp.int32, (16, 128), 1)
    sub = lax.broadcasted_iota(jnp.int32, (16, 128), 0)

    def place(offset, step):
        z_to, x_to = (z + offset) % 8, (x + step) % NX
        here = (x_to + y + z_to) % 2 == 0
        return z_to, x_to, here, jnp.where(here, y, side)

    def target(offset, here):
        start = pl.multiple_of(lane_group * 32 + jnp.where(here, 0, 16), 16)
        return keys.at[ORDER.index((8 - offset) % 8), pl.ds(start, 16)]

    def send_copy(offset, step):
        z_to, x_to, here, y_to = place(offset, step)
        return pltpu.make_async_remote_copy(
            send.at[offset, pl.ds(step * 16, 16)], target(offset, here), out_sem.at[offset],
            in_sem.at[ORDER.index((8 - offset) % 8)],
            device_id=device(x_to, z_to, owner_core(x_to), y_to), device_id_type=MESH
        )

    def own_copy():
        return pltpu.make_async_copy(send.at[0, pl.ds(0, 16)], target(0, True), own_sem)

    for half in range(2):
        offsets = ORDER[4 * half:4 * half + 4]
        pick = jnp.concatenate(
            [
                jnp.concatenate(
                    [
                        jnp.where(iota_slot + o * 64 == slot[b:b + 1, :], 1.0, 0.0).astype(jnp.bfloat16)
                        for b in range(8)
                    ],
                    axis=1,
                )
                for o in offsets
            ],
            axis=0,
        )
        picked = jnp.dot(pick, emb[...], preferred_element_type=jnp.float32)
        scale = lax.rsqrt(jnp.sum(picked * picked, axis=1, keepdims=True) + EPSILON)
        normed = (picked * scale).astype(jnp.bfloat16)
        for n, o in enumerate(offsets):
            send[o] = normed[n * 64:(n + 1) * 64, :]
            for step in range(NX):
                z_to, x_to, here, y_to = place(o, step)
                count = best_lane[pl.ds(16 * y_to + 2 * z_to + x_to // 2, 1), :]
                empty = (sub + jnp.where(here, 0, 16)).astype(jnp.float32) >= count
                first = n * 64 + step * 16
                head = normed[first:first + 16, :128].astype(jnp.float32)
                head = jnp.where(empty & (lane == 0), FLAG, head)
                send[o, step * 16:(step + 1) * 16, 0:128] = head.astype(jnp.bfloat16)
        if half == 0:
            @pl.when(is_owner)
            def _():
                pl.semaphore_wait(barrier, 31 + NY - 1)

            @pl.when(jnp.logical_not(is_owner))
            def _():
                pl.semaphore_wait(barrier, 32 + NY - 1)
        for o in offsets:
            for step in range(1, NX):
                send_copy(o, step).start()
            if o:
                send_copy(o, 0).start()
            else:
                @pl.when(is_owner)
                def _():
                    own_copy().start()

                @pl.when(jnp.logical_not(is_owner))
                def _():
                    send_copy(0, 0).start()

    lanes256 = lax.broadcasted_iota(jnp.int32, (1, 256), 1)
    dims = (((1,), (1,)), ((), ()))

    def compute(t):
        if t == 0:
            own_copy().wait()
        rows = pl.ds(0, 240 if t == 0 else 256)
        pltpu.make_async_remote_copy(
            keys.at[t, rows], keys.at[t, rows], out_sem.at[0], in_sem.at[t],
            device_id=device(x, z, 1 - core, y), device_id_type=MESH
        ).wait_recv()
        new = keys[t]
        z_new = (z + ORDER[t]) % 8
        flags = keys[t, :, 0:128].astype(jnp.float32)
        bias = jnp.where(flags[:, 0:1] > 2.0, OFF, 0.0)
        row_bias[t] = jnp.broadcast_to(bias, (256, 128))
        first = jnp.where(lax.broadcasted_iota(jnp.int32, (16, 128), 1) == 0, 1.0, 0.0)
        lane_flag = lax.dot_general(
            first.astype(jnp.bfloat16), keys[t, :, 0:128], dims, preferred_element_type=jnp.float32
        )[0:1, :]
        lane_bias = jnp.where(lane_flag > 2.0, OFF, 0.0)
        scores = lax.dot_general(new, new, dims, preferred_element_type=jnp.float32)
        key_i = lax.broadcasted_iota(jnp.int32, (256, 256), 0)
        query_i = lax.broadcasted_iota(jnp.int32, (256, 256), 1)
        bias2 = jnp.concatenate([row_bias[t], row_bias[t]], axis=1)
        scores = jnp.where(key_i < query_i, scores + bias2, OFF)
        top = jnp.max(scores.reshape(32, 8, 256), axis=0)
        for u in range(t):
            z_old = (z + ORDER[u]) % 8
            shift = jnp.where(z_old < z_new, 0, 64)
            scores = lax.dot_general(keys[u], new, dims, preferred_element_type=jnp.float32)
            bias2 = jnp.concatenate([row_bias[u], row_bias[u]], axis=1)
            for g in range(4):
                new_later = lanes256 >= 64 * g + shift
                part = scores[64 * g:64 * (g + 1), :]
                down = part + bias2[64 * g:64 * (g + 1), :] + jnp.where(new_later, 0.0, OFF)
                top = jnp.maximum(top, jnp.max(down.reshape(8, 8, 256), axis=0))
                across = part + (lane_bias + jnp.where(new_later, OFF, 0.0))
                across = jnp.maximum(across[:, :128], across[:, 128:])
                rows = pl.ds(64 * g, 64)
                if u == t - 1:
                    acc[u, rows, :] = across
                else:
                    acc[u, rows, :] = jnp.maximum(acc[u, rows, :], across)
        best_lane[64 + t:65 + t, :] = jnp.max(top[:, :128], axis=0, keepdims=True)
        best_lane[72 + t:73 + t, :] = jnp.max(top[:, 128:], axis=0, keepdims=True)

    @pl.when(is_owner)
    def _():
        for t in range(NZ):
            compute(t)
        for h in range(2):
            for t in range(NZ):
                row = jnp.maximum(best_lane[64 + 8 * h + t:65 + 8 * h + t, :], -1.0)
                if t < NZ - 1:
                    turned = acc[t, h * 128:(h + 1) * 128, :].T
                    row = jnp.maximum(row, jnp.max(turned, axis=0, keepdims=True))
                best[h, ORDER[t]] = row

    def back(cluster, offset, step):
        group = (lane_group + step) % GROUP
        return pltpu.make_async_remote_copy(
            best.at[group // 4, offset], table.at[cluster], back_send, back_recv,
            device_id={
                "rows": ((group // 2) * 8 + (z + offset) % 8) * 2 + group % 2,
                "help": (y + 2 - step // GROUP + NY) % NY,
            },
            device_id_type=MESH,
        )

    @pl.when(is_owner)
    def _():
        cluster = 16 * y + 2 * z + x // 2
        for offset in (4, 3, 5, 2, 6, 1, 7, 0):
            for step in range(32):
                if step != 16 or offset != 0:
                    back(cluster, offset, step).start()
        table[cluster] = best[lane_group // 4, 0]
        pltpu.make_async_remote_copy(
            table.at[pl.ds(0, 63)], table.at[pl.ds(0, 63)], back_send, back_recv,
            device_id=device(x, z, 1 - core, y), device_id_type=MESH
        ).wait_recv()

    @pl.when(jnp.logical_not(is_owner))
    def _():
        pltpu.make_async_remote_copy(
            table.at[pl.ds(0, 64)], table.at[pl.ds(0, 64)], back_send, back_recv,
            device_id=device(x, z, 1 - core, y), device_id_type=MESH
        ).wait_recv()

    values = table[0:64].reshape(64, 128)
    high = values.astype(jnp.bfloat16)
    rest = values - high.astype(jnp.float32)
    mid = rest.astype(jnp.bfloat16)
    low = (rest - mid.astype(jnp.float32)).astype(jnp.bfloat16)
    parts = jnp.concatenate([high, mid, low], axis=0)
    iota_lane = lax.broadcasted_iota(jnp.int32, (128, 128), 0)
    for b in range(8):
        hot = onehot[b * 64:(b + 1) * 64, :]
        hot3 = jnp.concatenate([hot, hot, hot], axis=0)
        looked = lax.dot_general(
            parts, hot3, (((0,), (0,)), ((), ())), preferred_element_type=jnp.float32
        )
        want = ranks[b:b + 1, :] + (lane_group % 4) * 32
        out_ref[b:b + 1, :] = jnp.sum(jnp.where(iota_lane == want, looked, 0.0), axis=0, keepdims=True)

    def sent(offset, rows):
        part = keys.at[0, pl.ds(0, rows)]
        pltpu.make_async_remote_copy(
            part, part, out_sem.at[offset], in_sem.at[0], device_id=device(x, z, 1 - core, y),
            device_id_type=MESH
        ).wait_send()

    for offset in range(1, NZ):
        sent(offset, 64)

    @pl.when(jnp.logical_not(is_owner))
    def _():
        sent(0, 64)

    @pl.when(is_owner)
    def _():
        sent(0, 48)

    @pl.when(is_owner)
    def _():
        pltpu.make_async_remote_copy(
            table.at[pl.ds(0, 255)], table.at[pl.ds(0, 255)], back_send, back_recv,
            device_id=device(x, z, 1 - core, y), device_id_type=MESH
        ).wait_send()


def local(embeddings, clusters):
    dma = pltpu.SemaphoreType.DMA
    vmem = pltpu.VMEM
    out = pl.pallas_call(
        kernel,
        out_shape=jax.ShapeDtypeStruct((8, 128), jnp.float32),
        in_specs=[
            pl.BlockSpec(memory_space=pltpu.HBM),
            pl.BlockSpec(memory_space=pltpu.VMEM),
        ],
        out_specs=pl.BlockSpec(memory_space=pltpu.VMEM),
        scratch_shapes=[
            vmem((ROWS, D), jnp.bfloat16),
            vmem((NZ, 64, D), jnp.bfloat16),
            vmem((NZ, BLOCK, D), jnp.bfloat16),
            vmem((NZ, BLOCK, 128), jnp.float32),
            vmem((NZ, BLOCK, 128), jnp.float32),
            vmem((80, 128), jnp.float32),
            vmem((8, 128), jnp.int32),
            vmem((512, 128), jnp.bfloat16),
            vmem((2, NZ, 1, 128), jnp.float32),
            vmem((256, 1, 128), jnp.float32),
            dma,
            dma((NZ,)),
            dma((NZ,)),
            dma,
            dma,
            dma,
        ],
        compiler_params=pltpu.CompilerParams(
            collective_id=0, has_side_effects=True, vmem_limit_bytes=60 << 20
        ),
    )(embeddings, clusters.reshape(8, 128))
    return out.reshape(ROWS)


def solution(mesh):
    placed = (P("rows", None), P("rows", None))
    return jax.shard_map(local, mesh=mesh, in_specs=placed, out_specs=P("rows"), check_vma=False)
```

```python
import jax
import jax.numpy as jnp
from jax import lax
from jax.experimental import pallas as pl
from jax.experimental.pallas import tpu as pltpu
from jax.sharding import PartitionSpec as P

EPSILON = 1e-06
MESH = pl.DeviceIdType.MESH
D = 1024
ROWS = 1024
MOST = 32
NX, NZ, NY, NK = 4, 8, 4, 2
GROUP = NX * NK
BLOCK = GROUP * MOST
ORDER = (0, 1, 7, 2, 6, 3, 5, 4)
FLAG = 4.0
OFF = -16.0


def kernel(emb_hbm, ids_ref, out_ref, emb, send, keys, acc, row_bias, best_lane, ranks,
           onehot, best, table,
           emb_sem, out_sem, in_sem, own_sem, back_send, back_recv):
    r = lax.axis_index("rows")
    y = lax.axis_index("help")
    x, z, core = r // 16, (r // 2) % 8, r % 2
    lane_group = x * 2 + core

    side = (y + 3 - 2 * core) % NY

    def owner_core(x_owner):
        return x_owner // 2

    is_owner = ((x + y + z) % 2 == 0) & (core == owner_core(x))

    def device(x_to, z_to, core_to, y_to):
        return {"rows": (x_to * 8 + z_to) * 2 + core_to, "help": y_to}

    load = pltpu.make_async_copy(emb_hbm, emb, emb_sem)
    load.start()

    barrier = pltpu.get_barrier_semaphore()
    @pl.when(is_owner)
    def _():
        for offset in (4, 3, 5, 2, 6, 1, 7, 0):
            z_to = (z + offset) % 8
            for step in range(NX):
                x_to = (x + 2 + step) % NX
                for core_to in range(NK):
                    @pl.when((offset != 0) | (step != 2) | (core_to != core))
                    def _():
                        pl.semaphore_signal(
                            barrier, inc=1, device_id=device(x_to, z_to, core_to, y),
                            device_id_type=MESH
                        )

                    pl.semaphore_signal(
                        barrier, inc=1,
                        device_id=device(x_to, z_to, core_to, (y + 1 + 2 * core_to) % NY),
                        device_id_type=MESH
                    )

    for step in range(1, NY):
        pl.semaphore_signal(
            barrier, inc=1, device_id={"help": (y + step) % NY}, device_id_type=MESH
        )

    iota_c = lax.broadcasted_iota(jnp.int32, (64, 128), 0)
    for b in range(8):
        hot = jnp.where(iota_c == ids_ref[b:b + 1, :], 1.0, 0.0).astype(jnp.bfloat16)
        onehot[b * 64:(b + 1) * 64, :] = hot
    tri_row = lax.broadcasted_iota(jnp.int32, (128, 256), 0)
    tri_col = lax.broadcasted_iota(jnp.int32, (128, 256), 1)
    tri = jnp.where((tri_row < tri_col) | (tri_col >= 128), 1.0, 0.0).astype(jnp.bfloat16)
    before = jnp.dot(onehot[...], tri, preferred_element_type=jnp.float32)
    base = jnp.zeros((64, 128), jnp.float32)
    for b in range(8):
        hot = onehot[b * 64:(b + 1) * 64, :].astype(jnp.float32)
        seen = before[b * 64:(b + 1) * 64, :128] + base
        rank = jnp.sum(hot * seen, axis=0, keepdims=True)
        ranks[b:b + 1, :] = rank.astype(jnp.int32)
        base = base + before[b * 64:(b + 1) * 64, 128:]
    best_lane[0:64, :] = base
    ids = ids_ref[...]
    plane, z_to, x_to = ids // 16, (ids // 2) % 8, (ids % 2) * 2 + (ids // 2 + ids // 16) % 2
    low = ranks[...] < 16
    slot = ((z_to - z + 8) % 8) * 64 + ((x_to - x + 4) % 4) * 16 + ranks[...] % 16
    slot = jnp.where(plane == jnp.where(low, y, side), slot, -1)

    load.wait()
    iota_slot = lax.broadcasted_iota(jnp.int32, (64, 128), 0)
    lane = lax.broadcasted_iota(jnp.int32, (16, 128), 1)
    sub = lax.broadcasted_iota(jnp.int32, (16, 128), 0)

    def place(offset, step):
        z_to, x_to = (z + offset) % 8, (x + step) % NX
        here = (x_to + y + z_to) % 2 == 0
        return z_to, x_to, here, jnp.where(here, y, side)

    def target(offset, here):
        start = pl.multiple_of(lane_group * 32 + jnp.where(here, 0, 16), 16)
        return keys.at[ORDER.index((8 - offset) % 8), pl.ds(start, 16)]

    def send_copy(offset, step):
        z_to, x_to, here, y_to = place(offset, step)
        return pltpu.make_async_remote_copy(
            send.at[offset, pl.ds(step * 16, 16)], target(offset, here), out_sem.at[offset],
            in_sem.at[ORDER.index((8 - offset) % 8)],
            device_id=device(x_to, z_to, owner_core(x_to), y_to), device_id_type=MESH
        )

    def own_copy():
        return pltpu.make_async_copy(send.at[0, pl.ds(0, 16)], target(0, True), own_sem)

    for half in range(2):
        offsets = ORDER[4 * half:4 * half + 4]
        pick = jnp.concatenate(
            [
                jnp.concatenate(
                    [
                        jnp.where(iota_slot + o * 64 == slot[b:b + 1, :], 1.0, 0.0).astype(jnp.bfloat16)
                        for b in range(8)
                    ],
                    axis=1,
                )
                for o in offsets
            ],
            axis=0,
        )
        picked = jnp.dot(pick, emb[...], preferred_element_type=jnp.float32)
        scale = lax.rsqrt(jnp.sum(picked * picked, axis=1, keepdims=True) + EPSILON)
        normed = (picked * scale).astype(jnp.bfloat16)
        for n, o in enumerate(offsets):
            send[o] = normed[n * 64:(n + 1) * 64, :]
            for step in range(NX):
                z_to, x_to, here, y_to = place(o, step)
                count = best_lane[pl.ds(16 * y_to + 2 * z_to + x_to // 2, 1), :]
                empty = (sub + jnp.where(here, 0, 16)).astype(jnp.float32) >= count
                first = n * 64 + step * 16
                head = normed[first:first + 16, :128].astype(jnp.float32)
                head = jnp.where(empty & (lane == 0), FLAG, head)
                send[o, step * 16:(step + 1) * 16, 0:128] = head.astype(jnp.bfloat16)
        if half == 0:
            @pl.when(is_owner)
            def _():
                pl.semaphore_wait(barrier, 31 + NY - 1)

            @pl.when(jnp.logical_not(is_owner))
            def _():
                pl.semaphore_wait(barrier, 32 + NY - 1)
        for o in offsets:
            for step in range(1, NX):
                send_copy(o, step).start()
            if o:
                send_copy(o, 0).start()
            else:
                @pl.when(is_owner)
                def _():
                    own_copy().start()

                @pl.when(jnp.logical_not(is_owner))
                def _():
                    send_copy(0, 0).start()

    lanes256 = lax.broadcasted_iota(jnp.int32, (1, 256), 1)
    dims = (((1,), (1,)), ((), ()))

    def compute(t):
        if t == 0:
            own_copy().wait()
        rows = pl.ds(0, 240 if t == 0 else 256)
        pltpu.make_async_remote_copy(
            keys.at[t, rows], keys.at[t, rows], out_sem.at[0], in_sem.at[t],
            device_id=device(x, z, 1 - core, y), device_id_type=MESH
        ).wait_recv()
        new = keys[t]
        z_new = (z + ORDER[t]) % 8
        flags = keys[t, :, 0:128].astype(jnp.float32)
        bias = jnp.where(flags[:, 0:1] > 2.0, OFF, 0.0)
        row_bias[t] = jnp.broadcast_to(bias, (256, 128))
        first = jnp.where(lax.broadcasted_iota(jnp.int32, (16, 128), 1) == 0, 1.0, 0.0)
        lane_flag = lax.dot_general(
            first.astype(jnp.bfloat16), keys[t, :, 0:128], dims, preferred_element_type=jnp.float32
        )[0:1, :]
        lane_bias = jnp.where(lane_flag > 2.0, OFF, 0.0)
        scores = lax.dot_general(new, new, dims, preferred_element_type=jnp.float32)
        key_i = lax.broadcasted_iota(jnp.int32, (256, 256), 0)
        query_i = lax.broadcasted_iota(jnp.int32, (256, 256), 1)
        bias2 = jnp.concatenate([row_bias[t], row_bias[t]], axis=1)
        scores = jnp.where(key_i < query_i, scores + bias2, OFF)
        top = jnp.max(scores.reshape(32, 8, 256), axis=0)
        for u in range(t):
            z_old = (z + ORDER[u]) % 8
            shift = jnp.where(z_old < z_new, 0, 64)
            scores = lax.dot_general(keys[u], new, dims, preferred_element_type=jnp.float32)
            bias2 = jnp.concatenate([row_bias[u], row_bias[u]], axis=1)
            for g in range(4):
                new_later = lanes256 >= 64 * g + shift
                part = scores[64 * g:64 * (g + 1), :]
                down = part + bias2[64 * g:64 * (g + 1), :] + jnp.where(new_later, 0.0, OFF)
                top = jnp.maximum(top, jnp.max(down.reshape(8, 8, 256), axis=0))
                across = part + (lane_bias + jnp.where(new_later, OFF, 0.0))
                across = jnp.maximum(across[:, :128], across[:, 128:])
                rows = pl.ds(64 * g, 64)
                if u == t - 1:
                    acc[u, rows, :] = across
                else:
                    acc[u, rows, :] = jnp.maximum(acc[u, rows, :], across)
        best_lane[64 + t:65 + t, :] = jnp.max(top[:, :128], axis=0, keepdims=True)
        best_lane[72 + t:73 + t, :] = jnp.max(top[:, 128:], axis=0, keepdims=True)

    @pl.when(is_owner)
    def _():
        for t in range(NZ):
            compute(t)
        for h in range(2):
            for t in range(NZ):
                row = jnp.maximum(best_lane[64 + 8 * h + t:65 + 8 * h + t, :], -1.0)
                if t < NZ - 1:
                    turned = acc[t, h * 128:(h + 1) * 128, :].T
                    row = jnp.maximum(row, jnp.max(turned, axis=0, keepdims=True))
                best[h, (z + ORDER[t]) % 8] = row

    def back(cluster, group, z_to, y_to):
        return pltpu.make_async_remote_copy(
            best.at[group // 4, z_to], table.at[cluster], back_send, back_recv,
            device_id=device(group // 2, z_to, group % 2, y_to), device_id_type=MESH
        )

    @pl.when(is_owner)
    def _():
        cluster = 16 * y + 2 * z + x // 2
        for z_to in range(NZ):
            for y_to in range(NY):
                for group in range(GROUP):
                    @pl.when((lane_group != group) | (z != z_to) | (y != y_to))
                    def _():
                        back(cluster, group, z_to, y_to).start()

        table[cluster] = best[lane_group // 4, z]
        pltpu.make_async_remote_copy(
            table.at[pl.ds(0, 63)], table.at[pl.ds(0, 63)], back_send, back_recv,
            device_id=device(x, z, 1 - core, y), device_id_type=MESH
        ).wait_recv()

    @pl.when(jnp.logical_not(is_owner))
    def _():
        pltpu.make_async_remote_copy(
            table.at[pl.ds(0, 64)], table.at[pl.ds(0, 64)], back_send, back_recv,
            device_id=device(x, z, 1 - core, y), device_id_type=MESH
        ).wait_recv()

    values = table[0:64].reshape(64, 128)
    high = values.astype(jnp.bfloat16)
    rest = values - high.astype(jnp.float32)
    mid = rest.astype(jnp.bfloat16)
    low = (rest - mid.astype(jnp.float32)).astype(jnp.bfloat16)
    parts = jnp.concatenate([high, mid, low], axis=0)
    iota_lane = lax.broadcasted_iota(jnp.int32, (128, 128), 0)
    for b in range(8):
        hot = onehot[b * 64:(b + 1) * 64, :]
        hot3 = jnp.concatenate([hot, hot, hot], axis=0)
        looked = lax.dot_general(
            parts, hot3, (((0,), (0,)), ((), ())), preferred_element_type=jnp.float32
        )
        want = ranks[b:b + 1, :] + (lane_group % 4) * 32
        out_ref[b:b + 1, :] = jnp.sum(jnp.where(iota_lane == want, looked, 0.0), axis=0, keepdims=True)

    def sent(offset, rows):
        part = keys.at[0, pl.ds(0, rows)]
        pltpu.make_async_remote_copy(
            part, part, out_sem.at[offset], in_sem.at[0], device_id=device(x, z, 1 - core, y),
            device_id_type=MESH
        ).wait_send()

    for offset in range(1, NZ):
        sent(offset, 64)

    @pl.when(jnp.logical_not(is_owner))
    def _():
        sent(0, 64)

    @pl.when(is_owner)
    def _():
        sent(0, 48)

    @pl.when(is_owner)
    def _():
        pltpu.make_async_remote_copy(
            table.at[pl.ds(0, 255)], table.at[pl.ds(0, 255)], back_send, back_recv,
            device_id=device(x, z, 1 - core, y), device_id_type=MESH
        ).wait_send()


def local(embeddings, clusters):
    dma = pltpu.SemaphoreType.DMA
    vmem = pltpu.VMEM
    out = pl.pallas_call(
        kernel,
        out_shape=jax.ShapeDtypeStruct((8, 128), jnp.float32),
        in_specs=[
            pl.BlockSpec(memory_space=pltpu.HBM),
            pl.BlockSpec(memory_space=pltpu.VMEM),
        ],
        out_specs=pl.BlockSpec(memory_space=pltpu.VMEM),
        scratch_shapes=[
            vmem((ROWS, D), jnp.bfloat16),
            vmem((NZ, 64, D), jnp.bfloat16),
            vmem((NZ, BLOCK, D), jnp.bfloat16),
            vmem((NZ, BLOCK, 128), jnp.float32),
            vmem((NZ, BLOCK, 128), jnp.float32),
            vmem((80, 128), jnp.float32),
            vmem((8, 128), jnp.int32),
            vmem((512, 128), jnp.bfloat16),
            vmem((2, NZ, 1, 128), jnp.float32),
            vmem((256, 1, 128), jnp.float32),
            dma,
            dma((NZ,)),
            dma((NZ,)),
            dma,
            dma,
            dma,
        ],
        compiler_params=pltpu.CompilerParams(
            collective_id=0, has_side_effects=True, vmem_limit_bytes=52 << 20
        ),
    )(embeddings, clusters.reshape(8, 128))
    return out.reshape(ROWS)


def solution(mesh):
    placed = (P("rows", None), P("rows", None))
    return jax.shard_map(local, mesh=mesh, in_specs=placed, out_specs=P("rows"), check_vma=False)
```

```python
import jax
import jax.numpy as jnp
from jax import lax
from jax.experimental import pallas as pl
from jax.experimental.pallas import tpu as pltpu
from jax.sharding import PartitionSpec as P

EPSILON = 1e-06
MESH = pl.DeviceIdType.MESH
D = 1024
ROWS = 1024
MOST = 32
NX, NZ, NY, NK = 4, 8, 4, 2
GROUP = NX * NK
BLOCK = GROUP * MOST
ORDER = (0, 1, 7, 2, 6, 3, 5, 4)
VMEM_LIMIT = 56553472
FLAG = 4.0
OFF = -16.0


def kernel(emb_hbm, ids_hbm, out_ref, ids_ref, emb, send, keys, acc, row_bias, best_lane, ranks,
           onehot, best, table,
           emb_sem, out_sem, in_sem, own_sem, back_send, back_recv):
    r = lax.axis_index("rows")
    y = lax.axis_index("help")
    x, z, core = r // 16, (r // 2) % 8, r % 2
    lane_group = x * 2 + core

    side = (y + 3 - 2 * core) % NY

    def owner_core(x_owner):
        return x_owner // 2

    is_owner = ((x + y + z) % 2 == 0) & (core == owner_core(x))

    def device(x_to, z_to, core_to, y_to):
        return {"rows": (x_to * 8 + z_to) * 2 + core_to, "help": y_to}

    load = pltpu.make_async_copy(emb_hbm, emb, emb_sem)
    load.start()
    load_ids = pltpu.make_async_copy(ids_hbm, ids_ref, own_sem)
    load_ids.start()

    barrier = pltpu.get_barrier_semaphore()
    for step in range(1, NY):
        pl.semaphore_signal(
            barrier, inc=1, device_id={"help": (y + step) % NY}, device_id_type=MESH
        )

    @pl.when(is_owner)
    def _():
        def ready(x_to, z_to, core_to, y_to):
            pl.semaphore_signal(
                barrier, inc=1, device_id=device(x_to, z_to, core_to, y_to), device_id_type=MESH
            )

        for offset in (4, 3, 5, 2, 6, 1, 7, 0):
            z_to = (z + offset) % 8
            for step in (2, 1, 3, 0):
                x_to = (x + step) % NX
                for core_to in range(NK):
                    ready(x_to, z_to, core_to, (y + 1 + 2 * core_to) % NY)
                    if offset or step:
                        ready(x_to, z_to, core_to, y)
        ready(x, z, 1 - core, y)

    load_ids.wait()
    iota_c = lax.broadcasted_iota(jnp.int32, (64, 128), 0)
    for b in range(8):
        hot = jnp.where(iota_c == ids_ref[b:b + 1, :], 1.0, 0.0).astype(jnp.bfloat16)
        onehot[b * 64:(b + 1) * 64, :] = hot
    tri_row = lax.broadcasted_iota(jnp.int32, (128, 256), 0)
    tri_col = lax.broadcasted_iota(jnp.int32, (128, 256), 1)
    tri = jnp.where((tri_row < tri_col) | (tri_col >= 128), 1.0, 0.0).astype(jnp.bfloat16)
    before = jnp.dot(onehot[...], tri, preferred_element_type=jnp.float32)
    base = jnp.zeros((64, 128), jnp.float32)
    for b in range(8):
        hot = onehot[b * 64:(b + 1) * 64, :].astype(jnp.float32)
        seen = before[b * 64:(b + 1) * 64, :128] + base
        rank = jnp.sum(hot * seen, axis=0, keepdims=True)
        ranks[b:b + 1, :] = rank.astype(jnp.int32)
        base = base + before[b * 64:(b + 1) * 64, 128:]
    best_lane[0:64, :] = base
    ids = ids_ref[...]
    plane, z_to, x_to = ids // 16, (ids // 2) % 8, (ids % 2) * 2 + (ids // 2 + ids // 16) % 2
    low = ranks[...] < 16
    slot = ((z_to - z + 8) % 8) * 64 + ((x_to - x + 4) % 4) * 16 + ranks[...] % 16
    slot = jnp.where(plane == jnp.where(low, y, side), slot, -1)

    load.wait()
    iota_slot = lax.broadcasted_iota(jnp.int32, (64, 128), 0)
    lane = lax.broadcasted_iota(jnp.int32, (16, 128), 1)
    sub = lax.broadcasted_iota(jnp.int32, (16, 128), 0)

    def place(offset, step):
        z_to, x_to = (z + offset) % 8, (x + step) % NX
        here = (x_to + y + z_to) % 2 == 0
        return z_to, x_to, here, jnp.where(here, y, side)

    def target(offset, here):
        start = pl.multiple_of(lane_group * 32 + jnp.where(here, 0, 16), 16)
        return keys.at[ORDER.index((8 - offset) % 8), pl.ds(start, 16)]

    def send_copy(offset, step):
        z_to, x_to, here, y_to = place(offset, step)
        return pltpu.make_async_remote_copy(
            send.at[offset, pl.ds(step * 16, 16)], target(offset, here), out_sem.at[offset],
            in_sem.at[ORDER.index((8 - offset) % 8)],
            device_id=device(x_to, z_to, owner_core(x_to), y_to), device_id_type=MESH
        )

    def own_copy():
        return pltpu.make_async_copy(send.at[0, pl.ds(0, 16)], target(0, True), own_sem)

    for half in range(1):
        offsets = ORDER
        pick = jnp.concatenate(
            [
                jnp.concatenate(
                    [
                        jnp.where(iota_slot + o * 64 == slot[b:b + 1, :], 1.0, 0.0).astype(jnp.bfloat16)
                        for b in range(8)
                    ],
                    axis=1,
                )
                for o in offsets
            ],
            axis=0,
        )
        picked = jnp.dot(pick, emb[...], preferred_element_type=jnp.float32)
        scale = lax.rsqrt(jnp.sum(picked * picked, axis=1, keepdims=True) + EPSILON)
        normed = (picked * scale).astype(jnp.bfloat16)
        for n, o in enumerate(offsets):
            send[o] = normed[n * 64:(n + 1) * 64, :]
            for step in range(NX):
                z_to, x_to, here, y_to = place(o, step)
                count = best_lane[pl.ds(16 * y_to + 2 * z_to + x_to // 2, 1), :]
                empty = (sub + jnp.where(here, 0, 16)).astype(jnp.float32) >= count
                first = n * 64 + step * 16
                head = normed[first:first + 16, :128].astype(jnp.float32)
                head = jnp.where(empty & (lane == 0), FLAG, head)
                send[o, step * 16:(step + 1) * 16, 0:128] = head.astype(jnp.bfloat16)
        if half == 0:
            @pl.when(is_owner)
            def _():
                pl.semaphore_wait(barrier, 31 + NY - 1)

            @pl.when(jnp.logical_not(is_owner))
            def _():
                pl.semaphore_wait(barrier, 32 + NY - 1)
        for o in offsets:
            for step in range(1, NX):
                send_copy(o, step).start()
            if o:
                send_copy(o, 0).start()
            else:
                @pl.when(is_owner)
                def _():
                    own_copy().start()

                @pl.when(jnp.logical_not(is_owner))
                def _():
                    send_copy(0, 0).start()

    lanes256 = lax.broadcasted_iota(jnp.int32, (1, 256), 1)
    dims = (((1,), (1,)), ((), ()))

    def compute(t):
        if t == 0:
            own_copy().wait()
        rows = pl.ds(0, 240 if t == 0 else 256)
        pltpu.make_async_remote_copy(
            keys.at[t, rows], keys.at[t, rows], out_sem.at[0], in_sem.at[t],
            device_id=device(x, z, 1 - core, y), device_id_type=MESH
        ).wait_recv()
        new = keys[t]
        z_new = (z + ORDER[t]) % 8
        flags = keys[t, :, 0:128].astype(jnp.float32)
        bias = jnp.where(flags[:, 0:1] > 2.0, OFF, 0.0)
        row_bias[t] = jnp.broadcast_to(bias, (256, 128))
        first = jnp.where(lax.broadcasted_iota(jnp.int32, (16, 128), 1) == 0, 1.0, 0.0)
        lane_flag = lax.dot_general(
            first.astype(jnp.bfloat16), keys[t, :, 0:128], dims, preferred_element_type=jnp.float32
        )[0:1, :]
        lane_bias = jnp.where(lane_flag > 2.0, OFF, 0.0)
        scores = lax.dot_general(new, new, dims, preferred_element_type=jnp.float32)
        key_i = lax.broadcasted_iota(jnp.int32, (256, 256), 0)
        query_i = lax.broadcasted_iota(jnp.int32, (256, 256), 1)
        bias2 = jnp.concatenate([row_bias[t], row_bias[t]], axis=1)
        scores = jnp.where(key_i < query_i, scores + bias2, OFF)
        top = jnp.max(scores.reshape(32, 8, 256), axis=0)
        for u in range(t):
            z_old = (z + ORDER[u]) % 8
            shift = jnp.where(z_old < z_new, 0, 64)
            scores = lax.dot_general(keys[u], new, dims, preferred_element_type=jnp.float32)
            bias2 = jnp.concatenate([row_bias[u], row_bias[u]], axis=1)
            for g in range(4):
                new_later = lanes256 >= 64 * g + shift
                part = scores[64 * g:64 * (g + 1), :]
                down = part + bias2[64 * g:64 * (g + 1), :] + jnp.where(new_later, 0.0, OFF)
                top = jnp.maximum(top, jnp.max(down.reshape(8, 8, 256), axis=0))
                across = part + (lane_bias + jnp.where(new_later, OFF, 0.0))
                across = jnp.maximum(across[:, :128], across[:, 128:])
                rows = pl.ds(64 * g, 64)
                if u == t - 1:
                    acc[u, rows, :] = across
                else:
                    acc[u, rows, :] = jnp.maximum(acc[u, rows, :], across)
        best_lane[64 + t:65 + t, :] = jnp.max(top[:, :128], axis=0, keepdims=True)
        best_lane[72 + t:73 + t, :] = jnp.max(top[:, 128:], axis=0, keepdims=True)

    @pl.when(is_owner)
    def _():
        for t in range(NZ):
            compute(t)
        for h in range(2):
            for t in range(NZ):
                row = jnp.maximum(best_lane[64 + 8 * h + t:65 + 8 * h + t, :], -1.0)
                if t < NZ - 1:
                    turned = acc[t, h * 128:(h + 1) * 128, :].T
                    row = jnp.maximum(row, jnp.max(turned, axis=0, keepdims=True))
                best[h, (z + ORDER[t]) % 8] = row

    def back(cluster, group, z_to, y_to):
        return pltpu.make_async_remote_copy(
            best.at[group // 4, z_to], table.at[cluster], back_send, back_recv,
            device_id=device(group // 2, z_to, group % 2, y_to), device_id_type=MESH
        )

    @pl.when(is_owner)
    def _():
        cluster = 16 * y + 2 * z + x // 2
        me = (y * NZ + z) * GROUP + lane_group
        places = [(z_to, y_to) for z_to in range(NZ) for y_to in range(NY)]
        for z_to, y_to in sorted(places, key=lambda p: p[0] + (1.5 if p[1] else 0.0)):
            for group in range(GROUP):
                @pl.when(me != (y_to * NZ + z_to) * GROUP + group)
                def _():
                    back(cluster, group, z_to, y_to).start()

        table[cluster] = best[lane_group // 4, z]
        pltpu.make_async_remote_copy(
            table.at[pl.ds(0, 63)], table.at[pl.ds(0, 63)], back_send, back_recv,
            device_id=device(x, z, 1 - core, y), device_id_type=MESH
        ).wait_recv()

    @pl.when(jnp.logical_not(is_owner))
    def _():
        pltpu.make_async_remote_copy(
            table.at[pl.ds(0, 64)], table.at[pl.ds(0, 64)], back_send, back_recv,
            device_id=device(x, z, 1 - core, y), device_id_type=MESH
        ).wait_recv()

    values = table[0:64].reshape(64, 128)
    high = values.astype(jnp.bfloat16)
    rest = values - high.astype(jnp.float32)
    mid = rest.astype(jnp.bfloat16)
    low = (rest - mid.astype(jnp.float32)).astype(jnp.bfloat16)
    parts = jnp.concatenate([high, mid, low], axis=0)
    iota_lane = lax.broadcasted_iota(jnp.int32, (128, 128), 0)
    for b in range(8):
        hot = onehot[b * 64:(b + 1) * 64, :]
        hot3 = jnp.concatenate([hot, hot, hot], axis=0)
        looked = lax.dot_general(
            parts, hot3, (((0,), (0,)), ((), ())), preferred_element_type=jnp.float32
        )
        want = ranks[b:b + 1, :] + (lane_group % 4) * 32
        out_ref[b:b + 1, :] = jnp.sum(jnp.where(iota_lane == want, looked, 0.0), axis=0, keepdims=True)

    def sent(offset, rows):
        part = keys.at[0, pl.ds(0, rows)]
        pltpu.make_async_remote_copy(
            part, part, out_sem.at[offset], in_sem.at[0], device_id=device(x, z, 1 - core, y),
            device_id_type=MESH
        ).wait_send()

    for offset in range(1, NZ):
        sent(offset, 64)

    @pl.when(jnp.logical_not(is_owner))
    def _():
        sent(0, 64)

    @pl.when(is_owner)
    def _():
        sent(0, 48)

    @pl.when(is_owner)
    def _():
        pltpu.make_async_remote_copy(
            table.at[pl.ds(0, 255)], table.at[pl.ds(0, 255)], back_send, back_recv,
            device_id=device(x, z, 1 - core, y), device_id_type=MESH
        ).wait_send()


def local(embeddings, clusters):
    dma = pltpu.SemaphoreType.DMA
    vmem = pltpu.VMEM
    out = pl.pallas_call(
        kernel,
        out_shape=jax.ShapeDtypeStruct((8, 128), jnp.float32),
        in_specs=[
            pl.BlockSpec(memory_space=pltpu.HBM),
            pl.BlockSpec(memory_space=pltpu.HBM),
        ],
        out_specs=pl.BlockSpec(memory_space=pltpu.VMEM),
        scratch_shapes=[
            vmem((8, 128), jnp.int32),
            vmem((ROWS, D), jnp.bfloat16),
            vmem((NZ, 64, D), jnp.bfloat16),
            vmem((NZ, BLOCK, D), jnp.bfloat16),
            vmem((NZ, BLOCK, 128), jnp.float32),
            vmem((NZ, BLOCK, 128), jnp.float32),
            vmem((80, 128), jnp.float32),
            vmem((8, 128), jnp.int32),
            vmem((512, 128), jnp.bfloat16),
            vmem((2, NZ, 1, 128), jnp.float32),
            vmem((256, 1, 128), jnp.float32),
            dma,
            dma((NZ,)),
            dma((NZ,)),
            dma,
            dma,
            dma,
        ],
        compiler_params=pltpu.CompilerParams(
            collective_id=0, has_side_effects=True, vmem_limit_bytes=VMEM_LIMIT
        ),
    )(embeddings, clusters.reshape(8, 128))
    return out.reshape(ROWS)


def solution(mesh):
    placed = (P("rows", None), P("rows", None))
    return jax.shard_map(local, mesh=mesh, in_specs=placed, out_specs=P("rows"), check_vma=False)
```

```python
import jax
import jax.numpy as jnp
from jax import lax
from jax.experimental import pallas as pl
from jax.experimental.pallas import tpu as pltpu
from jax.sharding import PartitionSpec as P

EPSILON = 1e-06
MESH = pl.DeviceIdType.MESH
D = 1024
ROWS = 1024
MOST = 32
NX, NZ, NY, NK = 4, 8, 4, 2
GROUP = NX * NK
BLOCK = GROUP * MOST
ORDER = (0, 1, 7, 2, 6, 3, 5, 4)
VMEM_LIMIT = 56553472
FLAG = 4.0
OFF = -16.0


def kernel(emb_hbm, ids_hbm, out_ref, ids_ref, emb, send, keys, acc, row_bias, best_lane, ranks,
           onehot, best, head, table,
           emb_sem, out_sem, in_sem, own_sem, back_send, back_recv):
    r = lax.axis_index("rows")
    y = lax.axis_index("help")
    x, z, core = r // 16, (r // 2) % 8, r % 2
    lane_group = x * 2 + core

    side = (y + 3 - 2 * core) % NY

    def owner_core(x_owner):
        return x_owner // 2

    is_owner = ((x + y + z) % 2 == 0) & (core == owner_core(x))

    def device(x_to, z_to, core_to, y_to):
        return {"rows": (x_to * 8 + z_to) * 2 + core_to, "help": y_to}

    load = pltpu.make_async_copy(emb_hbm, emb, emb_sem)
    load.start()
    load_ids = pltpu.make_async_copy(ids_hbm, ids_ref, own_sem)
    load_ids.start()

    barrier = pltpu.get_barrier_semaphore()
    for step in range(1, NY):
        pl.semaphore_signal(
            barrier, inc=1, device_id={"help": (y + step) % NY}, device_id_type=MESH
        )

    @pl.when(is_owner)
    def _():
        def ready(x_to, z_to, core_to, y_to):
            pl.semaphore_signal(
                barrier, inc=1, device_id=device(x_to, z_to, core_to, y_to), device_id_type=MESH
            )

        for offset in (4, 3, 5, 2, 6, 1, 7, 0):
            z_to = (z + offset) % 8
            for step in (2, 1, 3, 0):
                x_to = (x + step) % NX
                for core_to in range(NK):
                    ready(x_to, z_to, core_to, (y + 1 + 2 * core_to) % NY)
                    if offset or step:
                        ready(x_to, z_to, core_to, y)
        ready(x, z, 1 - core, y)

    load_ids.wait()
    iota_c = lax.broadcasted_iota(jnp.int32, (64, 128), 0)
    for b in range(8):
        hot = jnp.where(iota_c == ids_ref[b:b + 1, :], 1.0, 0.0).astype(jnp.bfloat16)
        onehot[b * 64:(b + 1) * 64, :] = hot
    tri_row = lax.broadcasted_iota(jnp.int32, (128, 256), 0)
    tri_col = lax.broadcasted_iota(jnp.int32, (128, 256), 1)
    tri = jnp.where((tri_row < tri_col) | (tri_col >= 128), 1.0, 0.0).astype(jnp.bfloat16)
    before = jnp.dot(onehot[...], tri, preferred_element_type=jnp.float32)
    base = jnp.zeros((64, 128), jnp.float32)
    for b in range(8):
        hot = onehot[b * 64:(b + 1) * 64, :].astype(jnp.float32)
        seen = before[b * 64:(b + 1) * 64, :128] + base
        rank = jnp.sum(hot * seen, axis=0, keepdims=True)
        ranks[b:b + 1, :] = rank.astype(jnp.int32)
        base = base + before[b * 64:(b + 1) * 64, 128:]
    best_lane[0:64, :] = base
    ids = ids_ref[...]
    plane, z_to, x_to = ids // 16, (ids // 2) % 8, (ids % 2) * 2 + (ids // 2 + ids // 16) % 2
    low = ranks[...] < 16
    slot = ((z_to - z + 8) % 8) * 64 + ((x_to - x + 4) % 4) * 16 + ranks[...] % 16
    slot = jnp.where(plane == jnp.where(low, y, side), slot, -1)

    load.wait()
    iota_slot = lax.broadcasted_iota(jnp.int32, (64, 128), 0)
    lane = lax.broadcasted_iota(jnp.int32, (16, 128), 1)
    sub = lax.broadcasted_iota(jnp.int32, (16, 128), 0)

    def place(offset, step):
        z_to, x_to = (z + offset) % 8, (x + step) % NX
        here = (x_to + y + z_to) % 2 == 0
        return z_to, x_to, here, jnp.where(here, y, side)

    def target(offset, here):
        start = pl.multiple_of(lane_group * 32 + jnp.where(here, 0, 16), 16)
        return keys.at[ORDER.index((8 - offset) % 8), pl.ds(start, 16)]

    def send_copy(offset, step):
        z_to, x_to, here, y_to = place(offset, step)
        return pltpu.make_async_remote_copy(
            send.at[offset, pl.ds(step * 16, 16)], target(offset, here), out_sem.at[offset],
            in_sem.at[ORDER.index((8 - offset) % 8)],
            device_id=device(x_to, z_to, owner_core(x_to), y_to), device_id_type=MESH
        )

    def own_copy():
        return pltpu.make_async_copy(send.at[0, pl.ds(0, 16)], target(0, True), own_sem)

    for half in range(1):
        offsets = ORDER
        pick = jnp.concatenate(
            [
                jnp.concatenate(
                    [
                        jnp.where(iota_slot + o * 64 == slot[b:b + 1, :], 1.0, 0.0).astype(jnp.bfloat16)
                        for b in range(8)
                    ],
                    axis=1,
                )
                for o in offsets
            ],
            axis=0,
        )
        picked = jnp.dot(pick, emb[...], preferred_element_type=jnp.float32)
        scale = lax.rsqrt(jnp.sum(picked * picked, axis=1, keepdims=True) + EPSILON)
        normed = (picked * scale).astype(jnp.bfloat16)
        for n, o in enumerate(offsets):
            send[o] = normed[n * 64:(n + 1) * 64, :]
            for step in range(NX):
                z_to, x_to, here, y_to = place(o, step)
                count = best_lane[pl.ds(16 * y_to + 2 * z_to + x_to // 2, 1), :]
                empty = (sub + jnp.where(here, 0, 16)).astype(jnp.float32) >= count
                first = n * 64 + step * 16
                start = normed[first:first + 16, :128].astype(jnp.float32)
                start = jnp.where(empty & (lane == 0), FLAG, start)
                send[o, step * 16:(step + 1) * 16, 0:128] = start.astype(jnp.bfloat16)
        if half == 0:
            @pl.when(is_owner)
            def _():
                pl.semaphore_wait(barrier, 31 + NY - 1)

            @pl.when(jnp.logical_not(is_owner))
            def _():
                pl.semaphore_wait(barrier, 32 + NY - 1)
        for o in offsets:
            for step in range(1, NX):
                send_copy(o, step).start()
            if o:
                send_copy(o, 0).start()
            else:
                @pl.when(is_owner)
                def _():
                    own_copy().start()

                @pl.when(jnp.logical_not(is_owner))
                def _():
                    send_copy(0, 0).start()

    lanes256 = lax.broadcasted_iota(jnp.int32, (1, 256), 1)
    dims = (((1,), (1,)), ((), ()))

    def back(cluster, group, z_to, y_to):
        return pltpu.make_async_remote_copy(
            best.at[group // 4, z_to], table.at[cluster], back_send, back_recv,
            device_id=device(group // 2, z_to, group % 2, y_to), device_id_type=MESH
        )

    me = (y * NZ + z) * GROUP + lane_group
    cluster = 16 * y + 2 * z + x // 2

    def head_back(group, y_to):
        return pltpu.make_async_remote_copy(
            head.at[0], table.at[cluster], back_send, back_recv,
            device_id=device(0, 0, group, y_to), device_id_type=MESH
        )

    def compute(t):
        if t == 0:
            own_copy().wait()
        rows = pl.ds(0, 240 if t == 0 else 256)
        pltpu.make_async_remote_copy(
            keys.at[t, rows], keys.at[t, rows], out_sem.at[0], in_sem.at[t],
            device_id=device(x, z, 1 - core, y), device_id_type=MESH
        ).wait_recv()
        new = keys[t]
        z_new = (z + ORDER[t]) % 8
        flags = keys[t, :, 0:128].astype(jnp.float32)
        bias = jnp.where(flags[:, 0:1] > 2.0, OFF, 0.0)
        row_bias[t] = jnp.broadcast_to(bias, (256, 128))
        first = jnp.where(lax.broadcasted_iota(jnp.int32, (16, 128), 1) == 0, 1.0, 0.0)
        lane_flag = lax.dot_general(
            first.astype(jnp.bfloat16), keys[t, :, 0:128], dims, preferred_element_type=jnp.float32
        )[0:1, :]
        lane_bias = jnp.where(lane_flag > 2.0, OFF, 0.0)
        scores = lax.dot_general(new, new, dims, preferred_element_type=jnp.float32)
        key_i = lax.broadcasted_iota(jnp.int32, (256, 256), 0)
        query_i = lax.broadcasted_iota(jnp.int32, (256, 256), 1)
        bias2 = jnp.concatenate([row_bias[t], row_bias[t]], axis=1)
        scores = jnp.where(key_i < query_i, scores + bias2, OFF)
        top = jnp.max(scores.reshape(32, 8, 256), axis=0)
        if t == NZ - 1:
            @pl.when(z_new == 0)
            def _():
                head[0] = jnp.maximum(jnp.max(top[:, :128], axis=0, keepdims=True), -1.0)
                for y_to in range(NY):
                    for group in range(NK):
                        head_back(group, y_to).start()

        for u in range(t):
            z_old = (z + ORDER[u]) % 8
            shift = jnp.where(z_old < z_new, 0, 64)
            scores = lax.dot_general(keys[u], new, dims, preferred_element_type=jnp.float32)
            bias2 = jnp.concatenate([row_bias[u], row_bias[u]], axis=1)
            for g in range(4):
                new_later = lanes256 >= 64 * g + shift
                part = scores[64 * g:64 * (g + 1), :]
                down = part + bias2[64 * g:64 * (g + 1), :] + jnp.where(new_later, 0.0, OFF)
                top = jnp.maximum(top, jnp.max(down.reshape(8, 8, 256), axis=0))
                across = part + (lane_bias + jnp.where(new_later, OFF, 0.0))
                across = jnp.maximum(across[:, :128], across[:, 128:])
                rows = pl.ds(64 * g, 64)
                if u == t - 1:
                    acc[u, rows, :] = across
                else:
                    acc[u, rows, :] = jnp.maximum(acc[u, rows, :], across)
        best_lane[64 + t:65 + t, :] = jnp.max(top[:, :128], axis=0, keepdims=True)
        best_lane[72 + t:73 + t, :] = jnp.max(top[:, 128:], axis=0, keepdims=True)

    @pl.when(is_owner)
    def _():
        for t in range(NZ):
            if t == NZ - 1:
                @pl.when(z != NZ // 2)
                def _():
                    offset = (8 - z) % 8
                    at = jnp.where(offset < 4, jnp.maximum(2 * offset - 1, 0), 2 * (8 - offset))
                    head[0] = jnp.maximum(best_lane[pl.ds(64 + at, 1), :], -1.0)
                    for y_to in range(NY):
                        for group in range(NK):
                            @pl.when(me != y_to * NZ * GROUP + group)
                            def _():
                                head_back(group, y_to).start()

            compute(t)
        for h in range(2):
            for t in range(NZ):
                row = jnp.maximum(best_lane[64 + 8 * h + t:65 + 8 * h + t, :], -1.0)
                if t < NZ - 1:
                    turned = acc[t, h * 128:(h + 1) * 128, :].T
                    row = jnp.maximum(row, jnp.max(turned, axis=0, keepdims=True))
                best[h, (z + ORDER[t]) % 8] = row

    @pl.when(is_owner)
    def _():
        places = [(z_to, y_to) for z_to in range(NZ) for y_to in range(NY)]
        for z_to, y_to in sorted(places, key=lambda p: p[0] + (1.5 if p[1] else 0.0)):
            for group in range(GROUP):
                if z_to or group >= NK:
                    @pl.when(me != (y_to * NZ + z_to) * GROUP + group)
                    def _():
                        back(cluster, group, z_to, y_to).start()

        table[cluster] = best[lane_group // 4, z]
        pltpu.make_async_remote_copy(
            table.at[pl.ds(0, 63)], table.at[pl.ds(0, 63)], back_send, back_recv,
            device_id=device(x, z, 1 - core, y), device_id_type=MESH
        ).wait_recv()

    @pl.when(jnp.logical_not(is_owner))
    def _():
        pltpu.make_async_remote_copy(
            table.at[pl.ds(0, 64)], table.at[pl.ds(0, 64)], back_send, back_recv,
            device_id=device(x, z, 1 - core, y), device_id_type=MESH
        ).wait_recv()

    values = table[0:64].reshape(64, 128)
    high = values.astype(jnp.bfloat16)
    rest = values - high.astype(jnp.float32)
    mid = rest.astype(jnp.bfloat16)
    low = (rest - mid.astype(jnp.float32)).astype(jnp.bfloat16)
    parts = jnp.concatenate([high, mid, low], axis=0)
    iota_lane = lax.broadcasted_iota(jnp.int32, (128, 128), 0)
    for b in range(8):
        hot = onehot[b * 64:(b + 1) * 64, :]
        hot3 = jnp.concatenate([hot, hot, hot], axis=0)
        looked = lax.dot_general(
            parts, hot3, (((0,), (0,)), ((), ())), preferred_element_type=jnp.float32
        )
        want = ranks[b:b + 1, :] + (lane_group % 4) * 32
        out_ref[b:b + 1, :] = jnp.sum(jnp.where(iota_lane == want, looked, 0.0), axis=0, keepdims=True)

    def sent(offset, rows):
        part = keys.at[0, pl.ds(0, rows)]
        pltpu.make_async_remote_copy(
            part, part, out_sem.at[offset], in_sem.at[0], device_id=device(x, z, 1 - core, y),
            device_id_type=MESH
        ).wait_send()

    for offset in range(1, NZ):
        sent(offset, 64)

    @pl.when(jnp.logical_not(is_owner))
    def _():
        sent(0, 64)

    @pl.when(is_owner)
    def _():
        sent(0, 48)

    @pl.when(is_owner)
    def _():
        pltpu.make_async_remote_copy(
            table.at[pl.ds(0, 255)], table.at[pl.ds(0, 255)], back_send, back_recv,
            device_id=device(x, z, 1 - core, y), device_id_type=MESH
        ).wait_send()


def local(embeddings, clusters):
    dma = pltpu.SemaphoreType.DMA
    vmem = pltpu.VMEM
    out = pl.pallas_call(
        kernel,
        out_shape=jax.ShapeDtypeStruct((8, 128), jnp.float32),
        in_specs=[
            pl.BlockSpec(memory_space=pltpu.HBM),
            pl.BlockSpec(memory_space=pltpu.HBM),
        ],
        out_specs=pl.BlockSpec(memory_space=pltpu.VMEM),
        scratch_shapes=[
            vmem((8, 128), jnp.int32),
            vmem((ROWS, D), jnp.bfloat16),
            vmem((NZ, 64, D), jnp.bfloat16),
            vmem((NZ, BLOCK, D), jnp.bfloat16),
            vmem((NZ, BLOCK, 128), jnp.float32),
            vmem((NZ, BLOCK, 128), jnp.float32),
            vmem((80, 128), jnp.float32),
            vmem((8, 128), jnp.int32),
            vmem((512, 128), jnp.bfloat16),
            vmem((2, NZ, 1, 128), jnp.float32),
            vmem((1, 1, 128), jnp.float32),
            vmem((256, 1, 128), jnp.float32),
            dma,
            dma((NZ,)),
            dma((NZ,)),
            dma,
            dma,
            dma,
        ],
        compiler_params=pltpu.CompilerParams(
            collective_id=0, has_side_effects=True, vmem_limit_bytes=VMEM_LIMIT
        ),
    )(embeddings, clusters.reshape(8, 128))
    return out.reshape(ROWS)


def solution(mesh):
    placed = (P("rows", None), P("rows", None))
    return jax.shard_map(local, mesh=mesh, in_specs=placed, out_specs=P("rows"), check_vma=False)
```

```python
import jax
import jax.numpy as jnp
from jax import lax
from jax.experimental import pallas as pl
from jax.experimental.pallas import tpu as pltpu
from jax.sharding import PartitionSpec as P

EPSILON = 1e-06
MESH = pl.DeviceIdType.MESH
D = 1024
ROWS = 1024
MOST = 32
NX, NZ, NY, NK = 4, 8, 4, 2
GROUP = NX * NK
BLOCK = GROUP * MOST
ORDER = (0, 1, 7, 2, 6, 3, 5, 4)
VMEM_LIMIT = 56553472
FLAG = 4.0
OFF = -16.0


def kernel(emb_hbm, ids_hbm, out_ref, ids_ref, emb, send, keys, acc, row_bias, best_lane, ranks,
           onehot, best, head, table,
           emb_sem, out_sem, in_sem, own_sem, back_send, back_recv):
    r = lax.axis_index("rows")
    y = lax.axis_index("help")
    x, z, core = r // 16, (r // 2) % 8, r % 2
    lane_group = x * 2 + core

    side = (y + 3 - 2 * core) % NY

    def owner_core(x_owner):
        return x_owner // 2

    is_owner = ((x + y + z) % 2 == 0) & (core == owner_core(x))

    def device(x_to, z_to, core_to, y_to):
        return {"rows": (x_to * 8 + z_to) * 2 + core_to, "help": y_to}

    load = pltpu.make_async_copy(emb_hbm, emb, emb_sem)
    load.start()
    load_ids = pltpu.make_async_copy(ids_hbm, ids_ref, own_sem)
    load_ids.start()

    barrier = pltpu.get_barrier_semaphore()
    for step in range(1, NY):
        pl.semaphore_signal(
            barrier, inc=1, device_id={"help": (y + step) % NY}, device_id_type=MESH
        )

    @pl.when(is_owner)
    def _():
        def ready(x_to, z_to, core_to, y_to):
            pl.semaphore_signal(
                barrier, inc=1, device_id=device(x_to, z_to, core_to, y_to), device_id_type=MESH
            )

        for offset in (4, 3, 5, 2, 6, 1, 7, 0):
            z_to = (z + offset) % 8
            for step in (2, 1, 3, 0):
                x_to = (x + step) % NX
                for core_to in range(NK):
                    ready(x_to, z_to, core_to, (y + 1 + 2 * core_to) % NY)
                    if offset or step:
                        ready(x_to, z_to, core_to, y)
        ready(x, z, 1 - core, y)

    load_ids.wait()
    iota_c = lax.broadcasted_iota(jnp.int32, (64, 128), 0)
    for b in range(8):
        hot = jnp.where(iota_c == ids_ref[b:b + 1, :], 1.0, 0.0).astype(jnp.bfloat16)
        onehot[b * 64:(b + 1) * 64, :] = hot
    tri_row = lax.broadcasted_iota(jnp.int32, (128, 256), 0)
    tri_col = lax.broadcasted_iota(jnp.int32, (128, 256), 1)
    tri = jnp.where((tri_row < tri_col) | (tri_col >= 128), 1.0, 0.0).astype(jnp.bfloat16)
    before = jnp.dot(onehot[...], tri, preferred_element_type=jnp.float32)
    base = jnp.zeros((64, 128), jnp.float32)
    for b in range(8):
        hot = onehot[b * 64:(b + 1) * 64, :].astype(jnp.float32)
        seen = before[b * 64:(b + 1) * 64, :128] + base
        rank = jnp.sum(hot * seen, axis=0, keepdims=True)
        ranks[b:b + 1, :] = rank.astype(jnp.int32)
        base = base + before[b * 64:(b + 1) * 64, 128:]
    best_lane[0:64, :] = base
    ids = ids_ref[...]
    plane, z_to, x_to = ids // 16, (ids // 2) % 8, (ids % 2) * 2 + (ids // 2 + ids // 16) % 2
    low = ranks[...] < 16
    slot = ((z_to - z + 8) % 8) * 64 + ((x_to - x + 4) % 4) * 16 + ranks[...] % 16
    slot = jnp.where(plane == jnp.where(low, y, side), slot, -1)

    load.wait()
    iota_slot = lax.broadcasted_iota(jnp.int32, (64, 128), 0)
    lane = lax.broadcasted_iota(jnp.int32, (16, 128), 1)
    sub = lax.broadcasted_iota(jnp.int32, (16, 128), 0)

    def place(offset, step):
        z_to, x_to = (z + offset) % 8, (x + step) % NX
        here = (x_to + y + z_to) % 2 == 0
        return z_to, x_to, here, jnp.where(here, y, side)

    def target(offset, here):
        start = pl.multiple_of(lane_group * 32 + jnp.where(here, 0, 16), 16)
        return keys.at[ORDER.index((8 - offset) % 8), pl.ds(start, 16)]

    def send_copy(offset, step):
        z_to, x_to, here, y_to = place(offset, step)
        return pltpu.make_async_remote_copy(
            send.at[offset, pl.ds(step * 16, 16)], target(offset, here), out_sem.at[offset],
            in_sem.at[ORDER.index((8 - offset) % 8)],
            device_id=device(x_to, z_to, owner_core(x_to), y_to), device_id_type=MESH
        )

    def own_copy():
        return pltpu.make_async_copy(send.at[0, pl.ds(0, 16)], target(0, True), own_sem)

    for half in range(1):
        offsets = ORDER
        pick = jnp.concatenate(
            [
                jnp.concatenate(
                    [
                        jnp.where(iota_slot + o * 64 == slot[b:b + 1, :], 1.0, 0.0).astype(jnp.bfloat16)
                        for b in range(8)
                    ],
                    axis=1,
                )
                for o in offsets
            ],
            axis=0,
        )
        picked = jnp.dot(pick, emb[...], preferred_element_type=jnp.float32)
        scale = lax.rsqrt(jnp.sum(picked * picked, axis=1, keepdims=True) + EPSILON)
        normed = (picked * scale).astype(jnp.bfloat16)
        for n, o in enumerate(offsets):
            send[o] = normed[n * 64:(n + 1) * 64, :]
            for step in range(NX):
                z_to, x_to, here, y_to = place(o, step)
                count = best_lane[pl.ds(16 * y_to + 2 * z_to + x_to // 2, 1), :]
                empty = (sub + jnp.where(here, 0, 16)).astype(jnp.float32) >= count
                first = n * 64 + step * 16
                start = normed[first:first + 16, :128].astype(jnp.float32)
                start = jnp.where(empty & (lane == 0), FLAG, start)
                send[o, step * 16:(step + 1) * 16, 0:128] = start.astype(jnp.bfloat16)
        if half == 0:
            @pl.when(is_owner)
            def _():
                pl.semaphore_wait(barrier, 31 + NY - 1)

            @pl.when(jnp.logical_not(is_owner))
            def _():
                pl.semaphore_wait(barrier, 32 + NY - 1)
        for o in offsets:
            for step in range(1, NX):
                send_copy(o, step).start()
            if o:
                send_copy(o, 0).start()
            else:
                @pl.when(is_owner)
                def _():
                    own_copy().start()

                @pl.when(jnp.logical_not(is_owner))
                def _():
                    send_copy(0, 0).start()

    lanes256 = lax.broadcasted_iota(jnp.int32, (1, 256), 1)
    dims = (((1,), (1,)), ((), ()))

    def back(cluster, group, z_to, y_to):
        return pltpu.make_async_remote_copy(
            best.at[group // 4, z_to], table.at[cluster], back_send, back_recv,
            device_id=device(group // 2, z_to, group % 2, y_to), device_id_type=MESH
        )

    me = (y * NZ + z) * GROUP + lane_group
    cluster = 16 * y + 2 * z + x // 2

    def head_back(group, y_to):
        return pltpu.make_async_remote_copy(
            head.at[0], table.at[cluster], back_send, back_recv,
            device_id=device(0, 0, group, y_to), device_id_type=MESH
        )

    def compute(t):
        if t == 0:
            own_copy().wait()
        rows = pl.ds(0, 240 if t == 0 else 256)
        pltpu.make_async_remote_copy(
            keys.at[t, rows], keys.at[t, rows], out_sem.at[0], in_sem.at[t],
            device_id=device(x, z, 1 - core, y), device_id_type=MESH
        ).wait_recv()
        new = keys[t]
        z_new = (z + ORDER[t]) % 8
        flags = keys[t, :, 0:128].astype(jnp.float32)
        bias = jnp.where(flags[:, 0:1] > 2.0, OFF, 0.0)
        row_bias[t] = jnp.broadcast_to(bias, (256, 128))
        first = jnp.where(lax.broadcasted_iota(jnp.int32, (16, 128), 1) == 0, 1.0, 0.0)
        lane_flag = lax.dot_general(
            first.astype(jnp.bfloat16), keys[t, :, 0:128], dims, preferred_element_type=jnp.float32
        )[0:1, :]
        lane_bias = jnp.where(lane_flag > 2.0, OFF, 0.0)
        scores = lax.dot_general(new, new, dims, preferred_element_type=jnp.float32)
        key_i = lax.broadcasted_iota(jnp.int32, (256, 256), 0)
        query_i = lax.broadcasted_iota(jnp.int32, (256, 256), 1)
        bias2 = jnp.concatenate([row_bias[t], row_bias[t]], axis=1)
        scores = jnp.where(key_i < query_i, scores + bias2, OFF)
        top = jnp.max(scores.reshape(32, 8, 256), axis=0)
        if t == NZ - 1:
            @pl.when(z_new == 0)
            def _():
                head[0] = jnp.maximum(jnp.max(top[:, :128], axis=0, keepdims=True), -1.0)
                for y_to in range(NY):
                    for group in range(NK):
                        head_back(group, y_to).start()

        for u in range(t):
            z_old = (z + ORDER[u]) % 8
            shift = jnp.where(z_old < z_new, 0, 64)
            scores = lax.dot_general(keys[u], new, dims, preferred_element_type=jnp.float32)
            bias2 = jnp.concatenate([row_bias[u], row_bias[u]], axis=1)
            for g in range(4):
                new_later = lanes256 >= 64 * g + shift
                part = scores[64 * g:64 * (g + 1), :]
                down = part + bias2[64 * g:64 * (g + 1), :] + jnp.where(new_later, 0.0, OFF)
                top = jnp.maximum(top, jnp.max(down.reshape(8, 8, 256), axis=0))
                across = part + (lane_bias + jnp.where(new_later, OFF, 0.0))
                across = jnp.maximum(across[:, :128], across[:, 128:])
                rows = pl.ds(64 * g, 64)
                if u == t - 1:
                    acc[u, rows, :] = across
                else:
                    acc[u, rows, :] = jnp.maximum(acc[u, rows, :], across)
        best_lane[64 + t:65 + t, :] = jnp.max(top[:, :128], axis=0, keepdims=True)
        best_lane[72 + t:73 + t, :] = jnp.max(top[:, 128:], axis=0, keepdims=True)

    @pl.when(is_owner)
    def _():
        for t in range(NZ):
            if t == NZ - 1:
                @pl.when(z != NZ // 2)
                def _():
                    offset = (8 - z) % 8
                    at = jnp.where(offset < 4, jnp.maximum(2 * offset - 1, 0), 2 * (8 - offset))
                    head[0] = jnp.maximum(best_lane[pl.ds(64 + at, 1), :], -1.0)
                    for y_to in range(NY):
                        for group in range(NK):
                            @pl.when(me != y_to * NZ * GROUP + group)
                            def _():
                                head_back(group, y_to).start()

            compute(t)
        for h in range(2):
            for t in range(NZ):
                row = jnp.maximum(best_lane[64 + 8 * h + t:65 + 8 * h + t, :], -1.0)
                if t < NZ - 1:
                    turned = acc[t, h * 128:(h + 1) * 128, :].T
                    row = jnp.maximum(row, jnp.max(turned, axis=0, keepdims=True))
                best[h, (z + ORDER[t]) % 8] = row

    @pl.when(is_owner)
    def _():
        places = [(z_to, y_to) for z_to in range(NZ) for y_to in range(NY)]
        for z_to, y_to in sorted(places, key=lambda p: p[0] + (1.5 if p[1] else 0.0)):
            groups = range(0 if z_to else NK, GROUP)
            here = (z == z_to) & (y == y_to)

            @pl.when(jnp.logical_not(here))
            def _():
                for group in groups:
                    back(cluster, group, z_to, y_to).start()

            @pl.when(here)
            def _():
                for group in groups:
                    @pl.when(lane_group != group)
                    def _():
                        back(cluster, group, z_to, y_to).start()

        table[cluster] = best[lane_group // 4, z]
        pltpu.make_async_remote_copy(
            table.at[pl.ds(0, 63)], table.at[pl.ds(0, 63)], back_send, back_recv,
            device_id=device(x, z, 1 - core, y), device_id_type=MESH
        ).wait_recv()

    @pl.when(jnp.logical_not(is_owner))
    def _():
        pltpu.make_async_remote_copy(
            table.at[pl.ds(0, 64)], table.at[pl.ds(0, 64)], back_send, back_recv,
            device_id=device(x, z, 1 - core, y), device_id_type=MESH
        ).wait_recv()

    values = table[0:64].reshape(64, 128)
    high = values.astype(jnp.bfloat16)
    rest = values - high.astype(jnp.float32)
    mid = rest.astype(jnp.bfloat16)
    low = (rest - mid.astype(jnp.float32)).astype(jnp.bfloat16)
    parts = jnp.concatenate([high, mid, low], axis=0)
    iota_lane = lax.broadcasted_iota(jnp.int32, (128, 128), 0)
    for b in range(8):
        hot = onehot[b * 64:(b + 1) * 64, :]
        hot3 = jnp.concatenate([hot, hot, hot], axis=0)
        looked = lax.dot_general(
            parts, hot3, (((0,), (0,)), ((), ())), preferred_element_type=jnp.float32
        )
        want = ranks[b:b + 1, :] + (lane_group % 4) * 32
        out_ref[b:b + 1, :] = jnp.sum(jnp.where(iota_lane == want, looked, 0.0), axis=0, keepdims=True)

    def sent(offset, rows):
        part = keys.at[0, pl.ds(0, rows)]
        pltpu.make_async_remote_copy(
            part, part, out_sem.at[offset], in_sem.at[0], device_id=device(x, z, 1 - core, y),
            device_id_type=MESH
        ).wait_send()

    for offset in range(1, NZ):
        sent(offset, 64)

    @pl.when(jnp.logical_not(is_owner))
    def _():
        sent(0, 64)

    @pl.when(is_owner)
    def _():
        sent(0, 48)

    @pl.when(is_owner)
    def _():
        pltpu.make_async_remote_copy(
            table.at[pl.ds(0, 255)], table.at[pl.ds(0, 255)], back_send, back_recv,
            device_id=device(x, z, 1 - core, y), device_id_type=MESH
        ).wait_send()


def local(embeddings, clusters):
    dma = pltpu.SemaphoreType.DMA
    vmem = pltpu.VMEM
    out = pl.pallas_call(
        kernel,
        out_shape=jax.ShapeDtypeStruct((8, 128), jnp.float32),
        in_specs=[
            pl.BlockSpec(memory_space=pltpu.HBM),
            pl.BlockSpec(memory_space=pltpu.HBM),
        ],
        out_specs=pl.BlockSpec(memory_space=pltpu.VMEM),
        scratch_shapes=[
            vmem((8, 128), jnp.int32),
            vmem((ROWS, D), jnp.bfloat16),
            vmem((NZ, 64, D), jnp.bfloat16),
            vmem((NZ, BLOCK, D), jnp.bfloat16),
            vmem((NZ, BLOCK, 128), jnp.float32),
            vmem((NZ, BLOCK, 128), jnp.float32),
            vmem((80, 128), jnp.float32),
            vmem((8, 128), jnp.int32),
            vmem((512, 128), jnp.bfloat16),
            vmem((2, NZ, 1, 128), jnp.float32),
            vmem((1, 1, 128), jnp.float32),
            vmem((256, 1, 128), jnp.float32),
            dma,
            dma((NZ,)),
            dma((NZ,)),
            dma,
            dma,
            dma,
        ],
        compiler_params=pltpu.CompilerParams(
            collective_id=0, has_side_effects=True, vmem_limit_bytes=VMEM_LIMIT
        ),
    )(embeddings, clusters.reshape(8, 128))
    return out.reshape(ROWS)


def solution(mesh):
    placed = (P("rows", None), P("rows", None))
    return jax.shard_map(local, mesh=mesh, in_specs=placed, out_specs=P("rows"), check_vma=False)
```
